256 devices in a mesh: tm: 4 (over x), space: 64 (over z, y, core).
Axes of the slice: x: 4, y: 4, z: 8, core: 2. Of those that a mesh axis runs over, the one named last changes fastest.
Arguments:
- c_points: float32 [4, 8192, 1024], P('tm', 'space'), may hold values from -3 to 3
- source: float32 [8192, 1024], P('space'), may hold values from -2 to 2
Outputs:
- c_new: float32 [4, 8192, 1024], P('tm', 'space')
- fine_end: float32 [4, 8192, 1024], P('tm', 'space')
The draws below stay inside these ranges and needn't reach their ends.
All inputs are finite; a program needn't handle non-finite values.
Results may differ from the reference program's by a relative error of at most 0.00002.
Values sent between devices are 32-bit elements; how exact they have to be, the bound alone decides.
No kernel may reach another device: no remote copies, remote signals or barrier semaphores. Data moves between devices by JAX's collectives and lax.ppermute only.
A program may use at most 64 MiB of HBM per device.

```python
import jax
import jax.numpy as jnp
from jax import lax

COLS = 1024
STEPS_SLAB = 8
SLABS = 4
NX = 8192


def row_signs(key, row_count, block_rows):
    block_count = (row_count + block_rows - 1) // block_rows
    coin_flips = jax.random.bernoulli(key, 0.5, (block_count,))
    per_block = jnp.where(coin_flips, 1.0, -1.0).astype(jnp.float32)
    return per_block[jnp.arange(row_count) // block_rows]


def draw_c_points(key, part):
    key = jax.random.fold_in(key, 11)
    sign_key, level_key, jitter_key = jax.random.split(key, 3)
    sign_rows = row_signs(sign_key, NX, 32)
    level_field = jax.random.uniform(level_key, (NX, COLS), jnp.float32, 2.2, 3.0)
    jitter_field = 0.2 * jnp.clip(jax.random.normal(jitter_key, (SLABS, NX, COLS), jnp.float32), -2.0, 2.0)
    magnitude = jnp.clip(level_field[None] + jitter_field, 1.8, 3.0)
    return sign_rows[None, :, None] * magnitude


def draw_source(key, part):
    key = jax.random.fold_in(key, 23)
    sign_key, level_key = jax.random.split(key, 2)
    sign_rows = row_signs(sign_key, NX, 32)
    magnitude = jax.random.uniform(level_key, (NX, COLS), jnp.float32, 0.5, 2.0)
    return sign_rows[:, None] * magnitude


def setup_inputs(seed: int = 0) -> dict:
    seeds = jax.random.split(jax.random.key(seed), 3)
    return {
        "c_points": draw_c_points(jax.random.fold_in(seeds[2], 71), 0),
        "source": draw_source(jax.random.fold_in(seeds[2], 71), 0),
    }


ADVECT = 0.02
DIFFUSE = 0.01
FORCE = 0.05


def advance(current, upper_row, lower_row, forcing, factor):
    left_col = jnp.roll(current, 1, axis=1)
    right_col = jnp.roll(current, -1, axis=1)
    transport = jnp.maximum(current, 0.0) * ((current - upper_row) + (current - left_col)) + jnp.minimum(current, 0.0) * ((lower_row - current) + (right_col - current))
    laplace_term = upper_row + lower_row + left_col + right_col - 4.0 * current
    return current - factor * ADVECT * transport + factor * DIFFUSE * laplace_term + factor * FORCE * forcing


def padded_step(current, forcing, factor):
    padded = jnp.pad(current, ((1, 1), (0, 0)))
    return advance(current, padded[:-2], padded[2:], forcing, factor)


def fine_slab(current, forcing):
    for _ in range(STEPS_SLAB):
        current = padded_step(current, forcing, 1.0)
    return current


def reference(c_points, source):
    coarse_factor = float(STEPS_SLAB)
    defect = jax.vmap(lambda start: fine_slab(start, source) - padded_step(start, source, coarse_factor))(c_points)

    def linked(carry, piece):
        ending = padded_step(carry, source, coarse_factor) + piece
        return ending, (ending, carry)

    _, (c_new, starts) = lax.scan(linked, c_points[0], defect)
    fine_end = jax.vmap(lambda start: fine_slab(start, source))(starts)
    return c_new, fine_end
```

```python
import functools

import jax
import jax.numpy as jnp
from jax import lax
from jax.experimental import pallas as pl
from jax.experimental.pallas import tpu as pltpu
from jax.sharding import PartitionSpec as P

ADVECT = 0.02
DIFFUSE = 0.01
FORCE = 0.05
STEPS = 8
SLABS = 4
ROWS = 128
COLS = 1024
LANE = 128
TILES = COLS // LANE
HALO = 24
PAD = 8
REACH = STEPS
PART = (ROWS + 2 * REACH) // SLABS
BLOCK = PART + 4
FAR = REACH + 2


def increment(now, above, below, left, right, force):
    twice = now + now
    rear = above + left - twice
    ahead = below + right - twice
    gain = jnp.maximum(now, 0.0) + DIFFUSE
    return force + gain * rear + (gain - now) * ahead


def row_tile(state, start, lane_ids):
    now = [state[g, pl.ds(start, 8), :] for g in range(TILES)]
    above = [state[g, pl.ds(start - 1, 8), :] for g in range(TILES)]
    below = [state[g, pl.ds(start + 1, 8), :] for g in range(TILES)]
    fore = [pltpu.roll(x, 1, 1) for x in now]
    back = [pltpu.roll(x, LANE - 1, 1) for x in now]
    for g in range(TILES):
        left = jnp.where(lane_ids == 0, fore[g - 1], fore[g])
        right = jnp.where(lane_ids == LANE - 1, back[(g + 1) % TILES], back[g])
        yield g, now[g], above[g], below[g], left, right


def lanes():
    return lax.broadcasted_iota(jnp.int32, (8, LANE), 1)


def place():
    slab = lax.axis_index("tm")
    strip = lax.axis_index("space")
    up_mask = jnp.where(strip == 0, 0.0, 1.0)
    down_mask = jnp.where(strip == lax.axis_size("space") - 1, 0.0, 1.0)
    return slab, strip % 2, up_mask, down_mask


def defect_kernel(c_ref, s_ref, intra_ref, inter_ref, defect_ref, mine_ref, one_ref, two_ref, three_ref, force_ref, one, two, force, coarse):
    slab, odd, up_mask, down_mask = place()
    lane_ids = lanes()
    base = PAD + HALO

    def fill(target, scale, top, main, bottom, offset):
        for g in range(TILES):
            cut = pl.ds(g * LANE, LANE)
            for i in range(HALO // 8):
                rows = pl.ds(offset + 8 * i, 8)
                target[g, pl.ds(PAD + 8 * i, 8), :] = top[rows, cut] * (scale * up_mask)
                target[g, pl.ds(base + ROWS + 8 * i, 8), :] = bottom[rows, cut] * (scale * down_mask)
            if main is not None:
                for i in range(ROWS // 8):
                    target[g, pl.ds(base + 8 * i, 8), :] = main[pl.ds(8 * i, 8), cut] * scale

    c_scale, s_scale = ADVECT, ADVECT * FORCE

    @pl.when(odd == 1)
    def _():
        fill(one, c_scale, intra_ref, c_ref, inter_ref, 0)
        fill(force, s_scale, intra_ref, s_ref, inter_ref, HALO)

    @pl.when(odd == 0)
    def _():
        fill(one, c_scale, inter_ref, c_ref, intra_ref, 0)
        fill(force, s_scale, inter_ref, s_ref, intra_ref, HALO)

    count = (ROWS + 2 * HALO) // 8
    edge = HALO // 8

    def sweep(source, target, first, last, keep):
        for i in range(first, last):
            at = PAD + 8 * i
            for g, now, above, below, left, right in row_tile(source, at, lane_ids):
                inc = increment(now, above, below, left, right, force[g, pl.ds(at, 8), :])
                new = now + inc
                if keep:
                    coarse[g, pl.ds(at, 8), :] = now + 8.0 * inc
                if i < edge:
                    new = new * up_mask
                if i >= count - edge:
                    new = new * down_mask
                target[g, pl.ds(at, 8), :] = new

    sweep(one, two, 0, count, True)
    sweep(two, one, 1, count - 1, False)

    def pair(_, carry):
        sweep(one, two, 1, count - 1, False)
        sweep(two, one, 1, count - 1, False)
        return carry

    lax.fori_loop(0, STEPS // 2 - 1, pair, 0)
    first = jnp.where(slab == 0, 0.0, 1.0)
    for i in range(1, count - 1):
        rows = pl.ds(PAD + 8 * i, 8)
        for g in range(TILES):
            fine = one[g, rows, :]
            rough = coarse[g, rows, :]
            if i < edge:
                rough = rough * up_mask
            if i >= count - edge:
                rough = rough * down_mask
            two[g, rows, :] = fine - first * rough
            if edge <= i < count - edge:
                defect_ref[pl.ds(8 * (i - edge), 8), pl.ds(g * LANE, LANE)] = fine - rough

    for k, out in enumerate((mine_ref, one_ref, two_ref, three_ref)):
        start = base - FAR + PART * (slab ^ k)
        for i in range(BLOCK // 8):
            for g in range(TILES):
                cut = pl.ds(g * LANE, LANE)
                rows = pl.ds(start + 8 * i, 8)
                out[pl.ds(8 * i, 8), cut] = two[g, rows, :]
                if k == 0:
                    force_ref[g, pl.ds(8 * i, 8), :] = force[g, rows, :]


def chain_kernel(mine_ref, one_ref, two_ref, three_ref, force_ref, out0_ref, out1_ref, out2_ref, out3_ref, start1, start2, start3):
    slab, odd, up_mask, down_mask = place()
    lane_ids = lanes()
    boxes = (mine_ref, one_ref, two_ref, three_ref)
    outs = (out0_ref, out1_ref, out2_ref, out3_ref)
    origin = PART * slab - FAR
    row_ids = lax.broadcasted_iota(jnp.int32, (8, LANE), 0)

    def sweep(source, target, defect):
        for i in range(BLOCK // 8):
            at = PAD + 8 * i
            row = row_ids + (origin + 8 * i)
            mask = jnp.where(row < 0, up_mask, jnp.where(row >= ROWS, down_mask, 1.0))
            for g, now, above, below, left, right in row_tile(source, at, lane_ids):
                inc = increment(now, above, below, left, right, force_ref[g, pl.ds(8 * i, 8), :])
                new = now + 8.0 * inc + defect[pl.ds(8 * i, 8), pl.ds(g * LANE, LANE)]
                target[g, pl.ds(at, 8), :] = new * mask

    for t in range(SLABS):
        @pl.when(slab == t)
        def _(t=t):
            for i in range(BLOCK // 8):
                for g in range(TILES):
                    start1[g, pl.ds(PAD + 8 * i, 8), :] = boxes[t][pl.ds(8 * i, 8), pl.ds(g * LANE, LANE)]
            sweep(start1, start2, boxes[t ^ 1])
            sweep(start2, start3, boxes[t ^ 2])
            starts = (None, start1, start2, start3)
            for k in range(SLABS):
                begin = starts[max(t ^ k, 1)]
                for i in range(BLOCK // 8):
                    size = min(8, PART - 8 * i)
                    for g in range(TILES):
                        outs[k][pl.ds(8 * i, size), pl.ds(g * LANE, LANE)] = begin[g, pl.ds(PAD + 2 + 8 * i, size), :]


def fine_kernel(c_ref, s_ref, intra_ref, inter_ref, defect_ref, mine_ref, one_ref, two_ref, three_ref, new_ref, end_ref, one, two, force):
    slab, odd, up_mask, down_mask = place()
    lane_ids = lanes()
    base = PAD + REACH
    boxes = (mine_ref, one_ref, two_ref, three_ref)
    c_scale, s_scale = ADVECT, ADVECT * FORCE

    def fill(target, scale, top, main, bottom, offset):
        for g in range(TILES):
            cut = pl.ds(g * LANE, LANE)
            target[g, pl.ds(PAD, 8), :] = top[pl.ds(offset + HALO - 8, 8), cut] * (scale * up_mask)
            target[g, pl.ds(base + ROWS, 8), :] = bottom[pl.ds(offset, 8), cut] * (scale * down_mask)
            for i in range(ROWS // 8):
                target[g, pl.ds(base + 8 * i, 8), :] = main[pl.ds(8 * i, 8), cut] * scale

    @pl.when(odd == 1)
    def _():
        fill(force, s_scale, intra_ref, s_ref, inter_ref, HALO)

    @pl.when(odd == 0)
    def _():
        fill(force, s_scale, inter_ref, s_ref, intra_ref, HALO)

    @pl.when((slab == 0) & (odd == 1))
    def _():
        fill(one, c_scale, intra_ref, c_ref, inter_ref, 0)

    @pl.when((slab == 0) & (odd == 0))
    def _():
        fill(one, c_scale, inter_ref, c_ref, intra_ref, 0)

    for t in range(1, SLABS):
        @pl.when(slab == t)
        def _(t=t):
            for w in range(SLABS):
                for i in range(BLOCK // 8):
                    size = min(8, PART - 8 * i)
                    for g in range(TILES):
                        one[g, pl.ds(PAD + PART * w + 8 * i, size), :] = boxes[t ^ w][pl.ds(8 * i, size), pl.ds(g * LANE, LANE)]

    count = (ROWS + 2 * REACH) // 8

    def sweep(source, target, first):
        for i in range(count):
            at = PAD + 8 * i
            for g, now, above, below, left, right in row_tile(source, at, lane_ids):
                inc = increment(now, above, below, left, right, force[g, pl.ds(at, 8), :])
                new = now + inc
                if i == 0:
                    new = new * up_mask
                elif i == count - 1:
                    new = new * down_mask
                elif first:
                    cut = (pl.ds(8 * i - 8, 8), pl.ds(g * LANE, LANE))
                    new_ref[cut] = (now + 8.0 * inc + defect_ref[cut]) * (1.0 / ADVECT)
                target[g, pl.ds(at, 8), :] = new

    sweep(one, two, True)

    def pair(_, carry):
        sweep(two, one, False)
        sweep(one, two, False)
        return carry

    lax.fori_loop(0, STEPS // 2 - 1, pair, 0)
    for i in range(1, count - 1):
        at = PAD + 8 * i
        for g, now, above, below, left, right in row_tile(two, at, lane_ids):
            inc = increment(now, above, below, left, right, force[g, pl.ds(at, 8), :])
            end_ref[pl.ds(8 * i - 8, 8), pl.ds(g * LANE, LANE)] = (now + inc) * (1.0 / ADVECT)


def swap(array, axis, by):
    size = lax.axis_size(axis)
    return lax.ppermute(array, axis, [(i, i ^ by) for i in range(size)])


def call(kernel, outs, scratch):
    spec = pl.BlockSpec(memory_space=pltpu.VMEM)
    return pl.pallas_call(
        kernel,
        out_shape=[jax.ShapeDtypeStruct(shape, jnp.float32) for shape in outs],
        out_specs=[spec] * len(outs),
        scratch_shapes=[pltpu.VMEM(shape, jnp.float32) for shape in scratch],
        compiler_params=pltpu.CompilerParams(vmem_limit_bytes=32 * 1024 * 1024),
    )


def local(c_points, source):
    field = c_points[0]
    odd = lax.axis_index("space") % 2 == 1
    count = lax.axis_size("space")
    top = jnp.concatenate([field[:HALO], source[:HALO]])
    bottom = jnp.concatenate([field[-HALO:], source[-HALO:]])
    intra = swap(jnp.where(odd, top, bottom), "space", 1)
    across = [(i, (i + 1) % count) for i in range(1, count, 2)]
    inter = lax.ppermute(jnp.where(odd, bottom, top), "space", across + [(b, a) for a, b in across])

    wide = (TILES, ROWS + 2 * HALO + 2 * PAD, LANE)
    block = (BLOCK, COLS)
    defect, *boxes, force = call(
        defect_kernel,
        [(ROWS, COLS)] + [block] * 4 + [(TILES, BLOCK, LANE)],
        [wide] * 4,
    )(field, source, intra, inter)
    boxes = [boxes[0]] + [swap(boxes[k], "tm", k) for k in (1, 3, 2)]
    boxes = [boxes[0], boxes[1], boxes[3], boxes[2]]
    starts = call(
        chain_kernel, [(PART, COLS)] * 4, [(TILES, BLOCK + 2 * PAD, LANE)] * 3
    )(*boxes, force)
    starts = [starts[0]] + [swap(starts[k], "tm", k) for k in (1, 3, 2)]
    starts = [starts[0], starts[1], starts[3], starts[2]]
    middle = (TILES, ROWS + 2 * REACH + 2 * PAD, LANE)
    corrected, fine = call(
        fine_kernel, [(ROWS, COLS)] * 2, [middle] * 3
    )(field, source, intra, inter, defect, *starts)
    return corrected[None], fine[None]


def solution(mesh):
    return jax.shard_map(
        local,
        mesh=mesh,
        in_specs=(P("tm", "space", None), P("space", None)),
        out_specs=(P("tm", "space", None), P("tm", "space", None)),
        check_vma=False,
    )
```

```python
import functools

import jax
import jax.numpy as jnp
from jax import lax
from jax.experimental import pallas as pl
from jax.experimental.pallas import tpu as pltpu
from jax.sharding import PartitionSpec as P

ADVECT = 0.02
DIFFUSE = 0.01
FORCE = 0.05
STEPS = 8
SLABS = 4
ROWS = 128
COLS = 1024
LANE = 128
TILES = COLS // LANE
HALO = 24
PAD = 8
REACH = STEPS
PART = (ROWS + 2 * REACH) // SLABS
BLOCK = PART + 4
FAR = REACH + 2
RIM = 2 * HALO
SIDE = RIM + 2 * PAD


ORDERS = ((0, 2, 1, 3), (0, 2, 3, 1))


def increment(now, above, below, left, right, force):
    twice = now + now
    rear = above + left - twice
    ahead = below + right - twice
    gain = jnp.maximum(now, 0.0) + DIFFUSE
    return force + gain * rear + (gain - now) * ahead


def row_tile(state, start, lane_ids):
    now = [state[g, pl.ds(start, 8), :] for g in range(TILES)]
    above = [state[g, pl.ds(start - 1, 8), :] for g in range(TILES)]
    below = [state[g, pl.ds(start + 1, 8), :] for g in range(TILES)]
    for g in range(TILES):
        left = pltpu.roll(jnp.where(lane_ids == LANE - 1, now[g - 1], now[g]), 1, 1)
        right = pltpu.roll(jnp.where(lane_ids == 0, now[(g + 1) % TILES], now[g]), LANE - 1, 1)
        yield g, now[g], above[g], below[g], left, right


def lanes():
    return lax.broadcasted_iota(jnp.int32, (8, LANE), 1)


def parity():
    return lax.axis_index("space") % 2


def place():
    slab = lax.axis_index("tm")
    strip = lax.axis_index("space")
    up_mask = jnp.where(strip == 0, 0.0, 1.0)
    down_mask = jnp.where(strip == lax.axis_size("space") - 1, 0.0, 1.0)
    return slab, strip % 2, up_mask, down_mask


def pack_kernel(c_ref, s_ref, intra_ref, inter_ref, sems):
    odd = parity()
    low = pl.multiple_of((ROWS - HALO) * odd, 8)
    high = pl.multiple_of((ROWS - HALO) * (1 - odd), 8)
    copies = []
    for n, (source, at) in enumerate(((c_ref.at[0], 0), (s_ref, HALO))):
        for m, (target, start) in enumerate(((inter_ref, low), (intra_ref, high))):
            copies.append(
                pltpu.make_async_copy(
                    source.at[pl.ds(start, HALO)], target.at[pl.ds(at, HALO)], sems.at[2 * n + m]
                )
            )
    for copy in copies:
        copy.start()
    for copy in copies:
        copy.wait()


def load(target, at, source, start, count, scale):
    for i in range(count):
        for g in range(TILES):
            target[g, pl.ds(at + 8 * i, 8), :] = source[pl.ds(start + 8 * i, 8), pl.ds(g * LANE, LANE)] * scale


def sweep(source, target, force, tiles, lane_ids, coarse=None, masks=None):
    for at in tiles:
        for g, now, above, below, left, right in row_tile(source, at, lane_ids):
            inc = increment(now, above, below, left, right, force[g, pl.ds(at, 8), :])
            new = now + inc
            if coarse is not None:
                coarse[g, pl.ds(at, 8), :] = now + 8.0 * inc
            if masks and at in masks:
                new = new * masks[at]
            target[g, pl.ds(at, 8), :] = new


def partner(place):
    first, second = ORDERS[0][place], ORDERS[1][place]
    return first if first == second else jnp.where(parity() == 0, first, second)


def inner_kernel(c_ref, s_ref, defect_ref, gift_ref, force_ref, one, two, coarse):
    slab = lax.axis_index("tm")
    lane_ids = lanes()
    count = ROWS // 8
    load(one, PAD, c_ref, 0, count, ADVECT)
    load(force_ref, PAD, s_ref, 0, count, ADVECT * FORCE)
    tiles = [PAD + 8 * i for i in range(count)]
    sweep(one, two, force_ref, tiles, lane_ids, coarse)
    sweep(two, one, force_ref, tiles, lane_ids)

    def pair(_, carry):
        sweep(one, two, force_ref, tiles, lane_ids)
        sweep(two, one, force_ref, tiles, lane_ids)
        return carry

    lax.fori_loop(0, STEPS // 2 - 1, pair, 0)
    first = jnp.where(slab == 0, 0.0, 1.0)
    for i in range(1, count - 1):
        rows = pl.ds(PAD + 8 * i, 8)
        for g in range(TILES):
            fine = one[g, rows, :]
            rough = coarse[g, rows, :]
            gift_ref[g, rows, :] = fine - first * rough
            defect_ref[pl.ds(8 * i, 8), pl.ds(g * LANE, LANE)] = fine - rough


def rim_kernel(c_ref, s_ref, intra_ref, inter_ref, inner_gift_ref, inner_force_ref, defect_ref, mine_ref, one_ref, two_ref, three_ref, block_ref, one, two, force, coarse, gift, wide_force):
    slab, odd, up_mask, down_mask = place()
    lane_ids = lanes()
    low, high = PAD, SIDE + PAD
    third = HALO // 8

    def fill(target, scale, top, main, bottom, offset):
        load(target, low, top, offset, third, scale * up_mask)
        load(target, low + HALO, main, 0, third, scale)
        load(target, high, main, ROWS - HALO, third, scale)
        load(target, high + HALO, bottom, offset, third, scale * down_mask)

    @pl.when(odd == 1)
    def _():
        fill(one, ADVECT, intra_ref, c_ref, inter_ref, 0)
        fill(force, ADVECT * FORCE, intra_ref, s_ref, inter_ref, HALO)

    @pl.when(odd == 0)
    def _():
        fill(one, ADVECT, inter_ref, c_ref, intra_ref, 0)
        fill(force, ADVECT * FORCE, inter_ref, s_ref, intra_ref, HALO)

    def tiles(first, last):
        upper = [low + 8 * i for i in range(first, last)]
        lower = [high + 8 * i for i in range(2 * third - last, 2 * third - first)]
        return upper + lower

    masks = {low + 8 * i: up_mask for i in range(third)}
    masks.update({high + HALO + 8 * i: down_mask for i in range(third)})
    sweep(one, two, force, tiles(0, 6), lane_ids, coarse, masks)
    sweep(two, one, force, tiles(1, 6), lane_ids, None, masks)
    sweep(one, two, force, tiles(1, 6), lane_ids, None, masks)
    sweep(two, one, force, tiles(1, 5), lane_ids, None, masks)

    def pair(_, carry):
        sweep(one, two, force, tiles(1, 5), lane_ids, None, masks)
        sweep(two, one, force, tiles(1, 5), lane_ids, None, masks)
        return carry

    lax.fori_loop(0, STEPS // 2 - 2, pair, 0)
    first = jnp.where(slab == 0, 0.0, 1.0)
    base = 2 * REACH
    for g in range(TILES):
        for i in range(1, ROWS // 8 - 1):
            gift[g, pl.ds(base + 8 * i, 8), :] = inner_gift_ref[g, pl.ds(PAD + 8 * i, 8), :]
        for i in range(ROWS // 8):
            wide_force[g, pl.ds(base + 8 * i, 8), :] = inner_force_ref[g, pl.ds(PAD + 8 * i, 8), :]
        for i in range(2):
            wide_force[g, pl.ds(8 * i, 8), :] = force[g, pl.ds(low + 8 + 8 * i, 8), :]
            wide_force[g, pl.ds(base + ROWS + 8 * i, 8), :] = force[g, pl.ds(high + HALO + 8 * i, 8), :]
    for n, at in enumerate([low + 8, low + 16, low + 24, high + 16, high + 24, high + 32]):
        rows = pl.ds(at, 8)
        place_at = 8 * n if n < 3 else base + ROWS - 8 + 8 * (n - 3)
        for g in range(TILES):
            fine = one[g, rows, :]
            rough = coarse[g, rows, :]
            if at in masks:
                rough = rough * masks[at]
            gift[g, pl.ds(place_at, 8), :] = fine - first * rough
            if at == low + HALO:
                defect_ref[pl.ds(0, 8), pl.ds(g * LANE, LANE)] = fine - rough
            if at == high + HALO - 8:
                defect_ref[pl.ds(8, 8), pl.ds(g * LANE, LANE)] = fine - rough
    for k, out in enumerate((mine_ref, one_ref, two_ref, three_ref)):
        start = base - FAR + PART * (slab ^ partner(k))
        for i in range(BLOCK // 8):
            for g in range(TILES):
                rows = pl.ds(start + 8 * i, 8)
                out[pl.ds(8 * i, 8), pl.ds(g * LANE, LANE)] = gift[g, rows, :]
                if k == 0:
                    block_ref[g, pl.ds(8 * i, 8), :] = wide_force[g, rows, :]


def each_place(slab, odd, body):
    for t in range(SLABS):
        for core in range(2):
            pl.when((slab == t) & (odd == core))(functools.partial(body, t, ORDERS[core]))


def chain_kernel(mine_ref, one_ref, two_ref, three_ref, force_ref, out0_ref, out1_ref, out2_ref, out3_ref, start1, start2, start3):
    slab, odd, up_mask, down_mask = place()
    lane_ids = lanes()
    boxes = (mine_ref, one_ref, two_ref, three_ref)
    outs = (out0_ref, out1_ref, out2_ref, out3_ref)
    row_ids = lax.broadcasted_iota(jnp.int32, (8, LANE), 0)
    origin = PART * slab - FAR

    def leap(source, target, defect):
        for i in range(BLOCK // 8):
            at = PAD + 8 * i
            row = row_ids + (origin + 8 * i)
            mask = jnp.where(row < 0, up_mask, jnp.where(row >= ROWS, down_mask, 1.0))
            for g, now, above, below, left, right in row_tile(source, at, lane_ids):
                inc = increment(now, above, below, left, right, force_ref[g, pl.ds(8 * i, 8), :])
                new = now + 8.0 * inc + defect[pl.ds(8 * i, 8), pl.ds(g * LANE, LANE)]
                target[g, pl.ds(at, 8), :] = new * mask

    def body(t, order):
        load(start1, PAD, boxes[order.index(t)], 0, BLOCK // 8, 1.0)
        leap(start1, start2, boxes[order.index(t ^ 1)])
        leap(start2, start3, boxes[order.index(t ^ 2)])
        starts = (None, start1, start2, start3)
        for k in range(SLABS):
            begin = starts[max(t ^ order[k], 1)]
            for i in range(BLOCK // 8):
                size = min(8, PART - 8 * i)
                for g in range(TILES):
                    outs[k][pl.ds(8 * i, size), pl.ds(g * LANE, LANE)] = begin[g, pl.ds(PAD + 2 + 8 * i, size), :]

    each_place(slab, odd, body)


def fine_kernel(c_ref, intra_ref, inter_ref, defect_ref, rim_defect_ref, inner_force_ref, mine_ref, one_ref, two_ref, three_ref, new_ref, end_ref, one, two, force):
    boxes = (mine_ref, one_ref, two_ref, three_ref)
    slab, odd, up_mask, down_mask = place()
    lane_ids = lanes()
    base = PAD + REACH
    last = base + ROWS

    def ends(target, scale, top, bottom, offset):
        load(target, PAD, top, offset + HALO - 8, 1, scale * up_mask)
        load(target, last, bottom, offset, 1, scale * down_mask)

    for g in range(TILES):
        for i in range(ROWS // 8):
            force[g, pl.ds(base + 8 * i, 8), :] = inner_force_ref[g, pl.ds(PAD + 8 * i, 8), :]

    @pl.when(odd == 1)
    def _():
        ends(force, ADVECT * FORCE, intra_ref, inter_ref, HALO)

    @pl.when(odd == 0)
    def _():
        ends(force, ADVECT * FORCE, inter_ref, intra_ref, HALO)

    @pl.when((slab == 0) & (odd == 1))
    def _():
        ends(one, ADVECT, intra_ref, inter_ref, 0)

    @pl.when((slab == 0) & (odd == 0))
    def _():
        ends(one, ADVECT, inter_ref, intra_ref, 0)

    @pl.when(slab == 0)
    def _():
        load(one, base, c_ref, 0, ROWS // 8, ADVECT)

    def body(t, order):
        for w in range(SLABS):
            source = boxes[order.index(t ^ w)]
            for i in range((PART + 7) // 8):
                size = min(8, PART - 8 * i)
                for g in range(TILES):
                    one[g, pl.ds(PAD + PART * w + 8 * i, size), :] = source[pl.ds(8 * i, size), pl.ds(g * LANE, LANE)]

    @pl.when(slab > 0)
    def _():
        each_place(slab, odd, body)

    tiles = [PAD + 8 * i for i in range((ROWS + 2 * REACH) // 8)]
    masks = {PAD: up_mask, last: down_mask}
    for at in tiles:
        for g, now, above, below, left, right in row_tile(one, at, lane_ids):
            inc = increment(now, above, below, left, right, force[g, pl.ds(at, 8), :])
            new = now + inc
            cut = pl.ds(g * LANE, LANE)
            if at in masks:
                new = new * masks[at]
            else:
                if at == base:
                    defect = rim_defect_ref[pl.ds(0, 8), cut]
                elif at == last - 8:
                    defect = rim_defect_ref[pl.ds(8, 8), cut]
                else:
                    defect = defect_ref[pl.ds(at - base, 8), cut]
                new_ref[pl.ds(at - base, 8), cut] = (now + 8.0 * inc + defect) * (1.0 / ADVECT)
            two[g, pl.ds(at, 8), :] = new

    def pair(_, carry):
        sweep(two, one, force, tiles, lane_ids, None, masks)
        sweep(one, two, force, tiles, lane_ids, None, masks)
        return carry

    lax.fori_loop(0, STEPS // 2 - 1, pair, 0)
    for at in tiles[1:-1]:
        for g, now, above, below, left, right in row_tile(two, at, lane_ids):
            inc = increment(now, above, below, left, right, force[g, pl.ds(at, 8), :])
            end_ref[pl.ds(at - base, 8), pl.ds(g * LANE, LANE)] = (now + inc) * (1.0 / ADVECT)


def swap(array, axis, by):
    size = lax.axis_size(axis)
    return lax.ppermute(array, axis, [(i, i ^ by) for i in range(size)])


def swap_all(boxes):
    count, width = lax.axis_size("tm"), lax.axis_size("space")
    received = [boxes[0]]
    for order in range(1, count):
        pairs = []
        for t in range(count):
            for strip in range(width):
                by = ORDERS[strip % 2][order]
                pairs.append((t * width + strip, (t ^ by) * width + strip))
        received.append(lax.ppermute(boxes[order], ("tm", "space"), pairs))
    return received


def call(kernel, outs, scratch):
    spec = pl.BlockSpec(memory_space=pltpu.VMEM)
    return pl.pallas_call(
        kernel,
        out_shape=[jax.ShapeDtypeStruct(shape, jnp.float32) for shape in outs],
        out_specs=[spec] * len(outs),
        scratch_shapes=[pltpu.VMEM(shape, jnp.float32) for shape in scratch],
        compiler_params=pltpu.CompilerParams(vmem_limit_bytes=24 * 1024 * 1024),
    )


def local(c_points, source):
    field = c_points[0]
    count = lax.axis_size("space")
    edges = jax.ShapeDtypeStruct((2 * HALO, COLS), jnp.float32)
    to_intra, to_inter = pl.pallas_call(
        pack_kernel,
        out_shape=[edges, edges],
        in_specs=[pl.BlockSpec(memory_space=pl.ANY)] * 2,
        out_specs=[pl.BlockSpec(memory_space=pltpu.VMEM)] * 2,
        scratch_shapes=[pltpu.SemaphoreType.DMA((4,))],
    )(c_points, source)
    pairs = []
    for t in range(lax.axis_size("tm")):
        for strip in range(count):
            if strip in (0, count - 1):
                mate = (t ^ 1) * count + strip
            else:
                mate = t * count + strip + (1 if strip % 2 else -1)
            pairs.append((t * count + strip, mate))
    inter = lax.ppermute(to_inter, ("tm", "space"), pairs)
    intra = swap(to_intra, "space", 1)

    wide = (TILES, ROWS + 2 * PAD, LANE)
    defect, gift, force = call(inner_kernel, [(ROWS, COLS), wide, wide], [wide] * 3)(field, source)
    narrow = (TILES, ROWS + 4 * REACH, LANE)
    rim_defect, *boxes, block_force = call(
        rim_kernel,
        [(16, COLS)] + [(BLOCK, COLS)] * 4 + [(TILES, BLOCK, LANE)],
        [(TILES, 2 * SIDE, LANE)] * 4 + [narrow] * 2,
    )(field, source, intra, inter, gift, force)
    starts = call(
        chain_kernel, [(PART, COLS)] * 4, [(TILES, BLOCK + 2 * PAD, LANE)] * 3
    )(*swap_all(boxes), block_force)
    middle = (TILES, ROWS + 2 * REACH + 2 * PAD, LANE)
    corrected, fine = call(fine_kernel, [(ROWS, COLS)] * 2, [middle] * 3)(
        field, intra, inter, defect, rim_defect, force, *swap_all(starts)
    )
    return corrected[None], fine[None]


def solution(mesh):
    return jax.shard_map(
        local,
        mesh=mesh,
        in_specs=(P("tm", "space", None), P("space", None)),
        out_specs=(P("tm", "space", None), P("tm", "space", None)),
        check_vma=False,
    )
```

```python
import functools

import jax
import jax.numpy as jnp
from jax import lax
from jax.experimental import pallas as pl
from jax.experimental.pallas import tpu as pltpu
from jax.sharding import PartitionSpec as P

ADVECT = 0.02
DIFFUSE = 0.01
FORCE = 0.05
STEPS = 8
SLABS = 4
ROWS = 128
COLS = 1024
LANE = 128
TILES = COLS // LANE
HALO = 24
PAD = 8
REACH = STEPS
PART = (ROWS + 2 * REACH) // SLABS
BLOCK = PART + 4
BOX = 48
FAR_BOX = 48
PIECE = BOX // 2
EDGE = PART // 2
FAR = REACH + 2
RIM_SLAB = 1
RIM = 2 * HALO
SIDE = RIM + 2 * PAD


ORDERS = ((0, 2, 1, 3), (0, 2, 3, 1))


def increment(now, above, below, left, right, force):
    twice = now + now
    rear = above + left - twice
    ahead = below + right - twice
    gain = jnp.maximum(now, 0.0) + DIFFUSE
    return force + gain * rear + (gain - now) * ahead


def row_tile(state, start, lane_ids):
    now = [state[g, pl.ds(start, 8), :] for g in range(TILES)]
    above = [state[g, pl.ds(start - 1, 8), :] for g in range(TILES)]
    below = [state[g, pl.ds(start + 1, 8), :] for g in range(TILES)]
    for g in range(TILES):
        left = pltpu.roll(jnp.where(lane_ids == LANE - 1, now[g - 1], now[g]), 1, 1)
        right = pltpu.roll(jnp.where(lane_ids == 0, now[(g + 1) % TILES], now[g]), LANE - 1, 1)
        yield g, now[g], above[g], below[g], left, right


def lanes():
    return lax.broadcasted_iota(jnp.int32, (8, LANE), 1)


def parity():
    return lax.axis_index("space") % 2


def place():
    slab = lax.axis_index("tm")
    strip = lax.axis_index("space")
    up_mask = jnp.where(strip == 0, 0.0, 1.0)
    down_mask = jnp.where(strip == lax.axis_size("space") - 1, 0.0, 1.0)
    return slab, strip % 2, up_mask, down_mask


def pack_kernel(c_ref, s_ref, intra_ref, inter_ref, sems):
    odd = parity()
    low = pl.multiple_of((ROWS - HALO) * odd, 8)
    high = pl.multiple_of((ROWS - HALO) * (1 - odd), 8)
    copies = []
    for n, (source, at) in enumerate(((c_ref.at[0], 0), (s_ref, HALO))):
        for m, (target, start) in enumerate(((inter_ref, low), (intra_ref, high))):
            copies.append(
                pltpu.make_async_copy(
                    source.at[pl.ds(start, HALO)], target.at[pl.ds(at, HALO)], sems.at[2 * n + m]
                )
            )
    for copy in copies:
        copy.start()
    for copy in copies:
        copy.wait()


def load(target, at, source, start, count, scale):
    for i in range(count):
        for g in range(TILES):
            target[g, pl.ds(at + 8 * i, 8), :] = source[pl.ds(start + 8 * i, 8), pl.ds(g * LANE, LANE)] * scale


def sweep(source, target, force, tiles, lane_ids, coarse=None, masks=None):
    for at in tiles:
        for g, now, above, below, left, right in row_tile(source, at, lane_ids):
            inc = increment(now, above, below, left, right, force[g, pl.ds(at, 8), :])
            new = now + inc
            if coarse is not None:
                coarse[g, pl.ds(at, 8), :] = now + 8.0 * inc
            if masks and at in masks:
                new = new * masks[at]
            target[g, pl.ds(at, 8), :] = new


def partner(place):
    first, second = ORDERS[0][place], ORDERS[1][place]
    return first if first == second else jnp.where(parity() == 0, first, second)


def inner_start(worker):
    return REACH + PART * jnp.where(worker > RIM_SLAB, worker - 1, jnp.where(worker == RIM_SLAB, 0, worker))


def inner_kernel(c_ref, s_ref, defect_ref, gift_ref, force_ref, far_ref, one, two, coarse):
    slab = lax.axis_index("tm")
    lane_ids = lanes()
    count = ROWS // 8
    load(one, PAD, c_ref, 0, count, ADVECT)
    load(force_ref, PAD, s_ref, 0, count, ADVECT * FORCE)
    tiles = [PAD + 8 * i for i in range(count)]
    sweep(one, two, force_ref, tiles, lane_ids, coarse)
    sweep(two, one, force_ref, tiles, lane_ids)

    def pair(_, carry):
        sweep(one, two, force_ref, tiles, lane_ids)
        sweep(two, one, force_ref, tiles, lane_ids)
        return carry

    lax.fori_loop(0, STEPS // 2 - 1, pair, 0)
    first = jnp.where(slab == 0, 0.0, 1.0)
    for i in range(1, count - 1):
        rows = pl.ds(PAD + 8 * i, 8)
        for g in range(TILES):
            fine = one[g, rows, :]
            rough = coarse[g, rows, :]
            gift_ref[g, rows, :] = fine - first * rough
            defect_ref[pl.ds(8 * i, 8), pl.ds(g * LANE, LANE)] = fine - rough
    start = PAD + inner_start(slab ^ 2)
    for i in range(FAR_BOX // 8):
        for g in range(TILES):
            far_ref[pl.ds(8 * i, 8), pl.ds(g * LANE, LANE)] = gift_ref[g, pl.ds(start + 8 * i, 8), :]


def rim_kernel(c_ref, s_ref, intra_ref, inter_ref, inner_gift_ref, inner_force_ref, defect_ref, mine_ref, one_ref, two_ref, block_ref, one, two, force, coarse, gift, wide_force):
    slab, odd, up_mask, down_mask = place()
    lane_ids = lanes()
    low, high = PAD, SIDE + PAD
    third = HALO // 8

    def fill(target, scale, top, main, bottom, offset):
        load(target, low, top, offset, third, scale * up_mask)
        load(target, low + HALO, main, 0, third, scale)
        load(target, high, main, ROWS - HALO, third, scale)
        load(target, high + HALO, bottom, offset, third, scale * down_mask)

    @pl.when(odd == 1)
    def _():
        fill(one, ADVECT, intra_ref, c_ref, inter_ref, 0)
        fill(force, ADVECT * FORCE, intra_ref, s_ref, inter_ref, HALO)

    @pl.when(odd == 0)
    def _():
        fill(one, ADVECT, inter_ref, c_ref, intra_ref, 0)
        fill(force, ADVECT * FORCE, inter_ref, s_ref, intra_ref, HALO)

    def tiles(first, last):
        upper = [low + 8 * i for i in range(first, last)]
        lower = [high + 8 * i for i in range(2 * third - last, 2 * third - first)]
        return upper + lower

    masks = {low + 8 * i: up_mask for i in range(third)}
    masks.update({high + HALO + 8 * i: down_mask for i in range(third)})
    sweep(one, two, force, tiles(0, 6), lane_ids, coarse, masks)
    sweep(two, one, force, tiles(1, 6), lane_ids, None, masks)
    sweep(one, two, force, tiles(1, 6), lane_ids, None, masks)
    sweep(two, one, force, tiles(1, 5), lane_ids, None, masks)

    def pair(_, carry):
        sweep(one, two, force, tiles(1, 5), lane_ids, None, masks)
        sweep(two, one, force, tiles(1, 5), lane_ids, None, masks)
        return carry

    lax.fori_loop(0, STEPS // 2 - 2, pair, 0)
    first = jnp.where(slab == 0, 0.0, 1.0)
    base = 2 * REACH
    for g in range(TILES):
        for i in range(1, ROWS // 8 - 1):
            gift[g, pl.ds(base + 8 * i, 8), :] = inner_gift_ref[g, pl.ds(PAD + 8 * i, 8), :]
        for i in range(ROWS // 8):
            wide_force[g, pl.ds(base + 8 * i, 8), :] = inner_force_ref[g, pl.ds(PAD + 8 * i, 8), :]
        for i in range(2):
            wide_force[g, pl.ds(8 * i, 8), :] = force[g, pl.ds(low + 8 + 8 * i, 8), :]
            wide_force[g, pl.ds(base + ROWS + 8 * i, 8), :] = force[g, pl.ds(high + HALO + 8 * i, 8), :]
    for n, at in enumerate([low + 8, low + 16, low + 24, high + 16, high + 24, high + 32]):
        rows = pl.ds(at, 8)
        place_at = 8 * n if n < 3 else base + ROWS - 8 + 8 * (n - 3)
        for g in range(TILES):
            fine = one[g, rows, :]
            rough = coarse[g, rows, :]
            if at in masks:
                rough = rough * masks[at]
            gift[g, pl.ds(place_at, 8), :] = fine - first * rough
            if at == low + HALO:
                defect_ref[pl.ds(0, 8), pl.ds(g * LANE, LANE)] = fine - rough
            if at == high + HALO - 8:
                defect_ref[pl.ds(8, 8), pl.ds(g * LANE, LANE)] = fine - rough
    for order, out in ((0, mine_ref), (2, one_ref), (3, two_ref)):
        worker = slab ^ partner(order)

        def cut(out, source, starts):
            for i in range(BOX // 8):
                at = starts[0] + 8 * i if i < PIECE // 8 else starts[1] + 8 * i - PIECE
                for g in range(TILES):
                    piece = source[g, pl.ds(at, 8), :]
                    if len(out.shape) == 3:
                        out[g, pl.ds(8 * i, 8), :] = piece
                    else:
                        out[pl.ds(8 * i, 8), pl.ds(g * LANE, LANE)] = piece

        def cut_all(starts, order=order, out=out):
            cut(out, gift, starts)
            if order == 0:
                cut(block_ref, wide_force, starts)

        @pl.when(worker == RIM_SLAB)
        def _(cut_all=cut_all):
            cut_all((base - FAR, base + ROWS + FAR - PIECE))

        @pl.when(worker != RIM_SLAB)
        def _(cut_all=cut_all, worker=worker):
            start = base + inner_start(worker)
            cut_all((start, start + PIECE))


def each_place(slab, odd, body):
    for t in range(SLABS):
        for core in range(2):
            pl.when((slab == t) & (odd == core))(functools.partial(body, t, ORDERS[core]))


def chain_kernel(mine_ref, one_ref, two_ref, three_ref, force_ref, out0_ref, out1_ref, out2_ref, out3_ref, start1, start2, start3):
    slab, odd, up_mask, down_mask = place()
    lane_ids = lanes()
    boxes = (mine_ref, one_ref, two_ref, three_ref)
    outs = (out0_ref, out1_ref, out2_ref, out3_ref)
    row_ids = lax.broadcasted_iota(jnp.int32, (8, LANE), 0)
    masks = {
        0: up_mask,
        1: jnp.where(row_ids < FAR - 8, up_mask, 1.0),
        4: jnp.where(row_ids >= 8 - (FAR - 8), down_mask, 1.0),
        5: down_mask,
    }

    def leap(source, target, defect, rim):
        for i in range((BOX if rim else BLOCK) // 8):
            at = PAD + 8 * i
            for g, now, above, below, left, right in row_tile(source, at, lane_ids):
                inc = increment(now, above, below, left, right, force_ref[g, pl.ds(8 * i, 8), :])
                new = now + 8.0 * inc + defect[pl.ds(8 * i, 8), pl.ds(g * LANE, LANE)]
                target[g, pl.ds(at, 8), :] = new * masks[i] if rim and i in masks else new

    def body(t, order):
        rim = t == RIM_SLAB
        load(start1, PAD, boxes[order.index(t)], 0, (BOX if rim else BLOCK) // 8, 1.0)
        leap(start1, start2, boxes[order.index(t ^ 1)], rim)
        leap(start2, start3, boxes[order.index(t ^ 2)], rim)
        starts = (None, start1, start2, start3)
        pieces = ((0, 2, EDGE), (EDGE, BOX - 2 - EDGE, EDGE)) if rim else ((0, 2, PART),)
        for k in range(SLABS):
            begin = starts[max(t ^ order[k], 1)]
            for to, at, rows in pieces:
                for i in range((rows + 7) // 8):
                    size = min(8, rows - 8 * i)
                    for g in range(TILES):
                        outs[k][pl.ds(to + 8 * i, size), pl.ds(g * LANE, LANE)] = begin[g, pl.ds(PAD + at + 8 * i, size), :]

    each_place(slab, odd, body)


def fine_kernel(c_ref, intra_ref, inter_ref, defect_ref, rim_defect_ref, inner_force_ref, mine_ref, one_ref, two_ref, three_ref, new_ref, end_ref, one, two, force):
    boxes = (mine_ref, one_ref, two_ref, three_ref)
    slab, odd, up_mask, down_mask = place()
    lane_ids = lanes()
    base = PAD + REACH
    last = base + ROWS

    def ends(target, scale, top, bottom, offset):
        load(target, PAD, top, offset + HALO - 8, 1, scale * up_mask)
        load(target, last, bottom, offset, 1, scale * down_mask)

    for g in range(TILES):
        for i in range(ROWS // 8):
            force[g, pl.ds(base + 8 * i, 8), :] = inner_force_ref[g, pl.ds(PAD + 8 * i, 8), :]

    @pl.when(odd == 1)
    def _():
        ends(force, ADVECT * FORCE, intra_ref, inter_ref, HALO)

    @pl.when(odd == 0)
    def _():
        ends(force, ADVECT * FORCE, inter_ref, intra_ref, HALO)

    @pl.when((slab == 0) & (odd == 1))
    def _():
        ends(one, ADVECT, intra_ref, inter_ref, 0)

    @pl.when((slab == 0) & (odd == 0))
    def _():
        ends(one, ADVECT, inter_ref, intra_ref, 0)

    @pl.when(slab == 0)
    def _():
        load(one, base, c_ref, 0, ROWS // 8, ADVECT)

    def body(t, order):
        for w in range(SLABS):
            source = boxes[order.index(t ^ w)]
            if w == RIM_SLAB:
                pieces = ((0, -REACH, EDGE), (EDGE, ROWS + REACH - EDGE, EDGE))
            else:
                pieces = ((0, EDGE - REACH + PART * (w - (w > RIM_SLAB)), PART),)
            for begin, row, rows in pieces:
                for i in range((rows + 7) // 8):
                    size = min(8, rows - 8 * i)
                    for g in range(TILES):
                        one[g, pl.ds(base + row + 8 * i, size), :] = source[pl.ds(begin + 8 * i, size), pl.ds(g * LANE, LANE)]

    @pl.when(slab > 0)
    def _():
        each_place(slab, odd, body)

    tiles = [PAD + 8 * i for i in range((ROWS + 2 * REACH) // 8)]
    masks = {PAD: up_mask, last: down_mask}
    for at in tiles:
        for g, now, above, below, left, right in row_tile(one, at, lane_ids):
            inc = increment(now, above, below, left, right, force[g, pl.ds(at, 8), :])
            new = now + inc
            cut = pl.ds(g * LANE, LANE)
            if at in masks:
                new = new * masks[at]
            else:
                if at == base:
                    defect = rim_defect_ref[pl.ds(0, 8), cut]
                elif at == last - 8:
                    defect = rim_defect_ref[pl.ds(8, 8), cut]
                else:
                    defect = defect_ref[pl.ds(at - base, 8), cut]
                new_ref[pl.ds(at - base, 8), cut] = (now + 8.0 * inc + defect) * (1.0 / ADVECT)
            two[g, pl.ds(at, 8), :] = new

    def pair(_, carry):
        sweep(two, one, force, tiles, lane_ids, None, masks)
        sweep(one, two, force, tiles, lane_ids, None, masks)
        return carry

    lax.fori_loop(0, STEPS // 2 - 1, pair, 0)
    for at in tiles[1:-1]:
        for g, now, above, below, left, right in row_tile(two, at, lane_ids):
            inc = increment(now, above, below, left, right, force[g, pl.ds(at, 8), :])
            end_ref[pl.ds(at - base, 8), pl.ds(g * LANE, LANE)] = (now + inc) * (1.0 / ADVECT)


def swap(array, axis, by):
    size = lax.axis_size(axis)
    return lax.ppermute(array, axis, [(i, i ^ by) for i in range(size)])


def swap_one(box, order):
    count, width = lax.axis_size("tm"), lax.axis_size("space")
    pairs = []
    for t in range(count):
        for strip in range(width):
            by = ORDERS[strip % 2][order]
            pairs.append((t * width + strip, (t ^ by) * width + strip))
    return lax.ppermute(box, ("tm", "space"), pairs)


def call(kernel, outs, scratch):
    spec = pl.BlockSpec(memory_space=pltpu.VMEM)
    return pl.pallas_call(
        kernel,
        out_shape=[jax.ShapeDtypeStruct(shape, jnp.float32) for shape in outs],
        out_specs=[spec] * len(outs),
        scratch_shapes=[pltpu.VMEM(shape, jnp.float32) for shape in scratch],
        compiler_params=pltpu.CompilerParams(vmem_limit_bytes=24 * 1024 * 1024),
    )


def local(c_points, source):
    field = c_points[0]
    count = lax.axis_size("space")
    edges = jax.ShapeDtypeStruct((2 * HALO, COLS), jnp.float32)
    to_intra, to_inter = pl.pallas_call(
        pack_kernel,
        out_shape=[edges, edges],
        in_specs=[pl.BlockSpec(memory_space=pl.ANY)] * 2,
        out_specs=[pl.BlockSpec(memory_space=pltpu.VMEM)] * 2,
        scratch_shapes=[pltpu.SemaphoreType.DMA((4,))],
    )(c_points, source)
    pairs = []
    for t in range(lax.axis_size("tm")):
        for strip in range(count):
            if strip in (0, count - 1):
                mate = (t ^ 1) * count + strip
            else:
                mate = t * count + strip + (1 if strip % 2 else -1)
            pairs.append((t * count + strip, mate))
    inter = lax.ppermute(to_inter, ("tm", "space"), pairs)
    intra = swap(to_intra, "space", 1)

    wide = (TILES, ROWS + 2 * PAD, LANE)
    defect, gift, force, far = call(
        inner_kernel, [(ROWS, COLS), wide, wide, (FAR_BOX, COLS)], [wide] * 3
    )(field, source)
    far = swap_one(far, 1)
    narrow = (TILES, ROWS + 4 * REACH, LANE)
    rim_defect, mine, one, two, block_force = call(
        rim_kernel,
        [(16, COLS)] + [(BOX, COLS)] * 3 + [(TILES, BOX, LANE)],
        [(TILES, 2 * SIDE, LANE)] * 4 + [narrow] * 2,
    )(field, source, intra, inter, gift, force)
    one, two = swap_one(one, 2), swap_one(two, 3)
    starts = call(
        chain_kernel, [(PART, COLS)] * 4, [(TILES, BOX + 2 * PAD, LANE)] * 3
    )(mine, far, one, two, block_force)
    starts = [starts[0]] + [swap_one(starts[order], order) for order in range(1, SLABS)]
    middle = (TILES, ROWS + 2 * REACH + 2 * PAD, LANE)
    corrected, fine = call(fine_kernel, [(ROWS, COLS)] * 2, [middle] * 3)(
        field, intra, inter, defect, rim_defect, force, *starts
    )
    return corrected[None], fine[None]


def solution(mesh):
    return jax.shard_map(
        local,
        mesh=mesh,
        in_specs=(P("tm", "space", None), P("space", None)),
        out_specs=(P("tm", "space", None), P("tm", "space", None)),
        check_vma=False,
    )
```

```python
import functools

import jax
import jax.numpy as jnp
from jax import lax
from jax.experimental import pallas as pl
from jax.experimental.pallas import tpu as pltpu
from jax.sharding import PartitionSpec as P

ADVECT = 0.02
DIFFUSE = 0.01
FORCE = 0.05
STEPS = 8
SLABS = 4
ROWS = 128
COLS = 1024
LANE = 128
TILES = COLS // LANE
HALO = 24
PAD = 8
REACH = STEPS
PART = (ROWS + 2 * REACH) // SLABS
BLOCK = PART + 4
BOX = 48
FAR_BOX = 64
CHUNK = 32
PIECE = BOX // 2
EDGE = PART // 2
FAR = REACH + 2
RIM_SLAB = 1
RIM = 2 * HALO
SIDE = RIM + 2 * PAD


ORDERS = ((0, 2, 1, 3), (0, 2, 3, 1))


def increment(now, above, below, left, right, force):
    twice = now + now
    rear = above + left - twice
    ahead = below + right - twice
    gain = jnp.maximum(now, 0.0) + DIFFUSE
    return force + gain * rear + (gain - now) * ahead


def row_tile(state, start, lane_ids):
    now = [state[g, pl.ds(start, 8), :] for g in range(TILES)]
    above = [state[g, pl.ds(start - 1, 8), :] for g in range(TILES)]
    below = [state[g, pl.ds(start + 1, 8), :] for g in range(TILES)]
    for g in range(TILES):
        left = pltpu.roll(jnp.where(lane_ids == LANE - 1, now[g - 1], now[g]), 1, 1)
        right = pltpu.roll(jnp.where(lane_ids == 0, now[(g + 1) % TILES], now[g]), LANE - 1, 1)
        yield g, now[g], above[g], below[g], left, right


def lanes():
    return lax.broadcasted_iota(jnp.int32, (8, LANE), 1)


def parity():
    return lax.axis_index("space") % 2


def place():
    slab = lax.axis_index("tm")
    strip = lax.axis_index("space")
    up_mask = jnp.where(strip == 0, 0.0, 1.0)
    down_mask = jnp.where(strip == lax.axis_size("space") - 1, 0.0, 1.0)
    return slab, strip % 2, up_mask, down_mask


def pack_kernel(c_ref, s_ref, intra_ref, inter_ref, far_ref, sems):
    odd = parity()
    low = pl.multiple_of((ROWS - HALO) * odd, 8)
    high = pl.multiple_of((ROWS - HALO) * (1 - odd), 8)
    middle = pl.multiple_of(FAR_BOX // 2 * inner_place(lax.axis_index("tm") ^ 2), 8)
    copies = []
    for n, (source, at) in enumerate(((c_ref.at[0], 0), (s_ref, HALO))):
        for m, (target, start) in enumerate(((inter_ref, low), (intra_ref, high))):
            copies.append(
                pltpu.make_async_copy(
                    source.at[pl.ds(start, HALO)], target.at[pl.ds(at, HALO)], sems.at[2 * n + m]
                )
            )
    copies.append(pltpu.make_async_copy(c_ref.at[0, pl.ds(middle, FAR_BOX)], far_ref, sems.at[4]))
    for copy in copies:
        copy.start()
    for copy in copies:
        copy.wait()


def load(target, at, source, start, count, scale):
    for i in range(count):
        for g in range(TILES):
            target[g, pl.ds(at + 8 * i, 8), :] = source[pl.ds(start + 8 * i, 8), pl.ds(g * LANE, LANE)] * scale


def sweep(source, target, force, tiles, lane_ids, coarse=None, masks=None):
    for at in tiles:
        for g, now, above, below, left, right in row_tile(source, at, lane_ids):
            inc = increment(now, above, below, left, right, force[g, pl.ds(at, 8), :])
            new = now + inc
            if coarse is not None:
                coarse[g, pl.ds(at, 8), :] = now + 8.0 * inc
            if masks and at in masks:
                new = new * masks[at]
            target[g, pl.ds(at, 8), :] = new


def partner(place):
    first, second = ORDERS[0][place], ORDERS[1][place]
    return first if first == second else jnp.where(parity() == 0, first, second)


def inner_place(worker):
    return jnp.where(worker > RIM_SLAB, worker - 1, 0)


def inner_start(worker):
    return REACH + PART * inner_place(worker)


def inner_kernel(c_ref, s_ref, defect_ref, gift_ref, force_ref, one, two, coarse):
    slab = lax.axis_index("tm")
    lane_ids = lanes()
    count = ROWS // 8
    load(one, PAD, c_ref, 0, count, ADVECT)
    load(force_ref, PAD, s_ref, 0, count, ADVECT * FORCE)
    tiles = [PAD + 8 * i for i in range(count)]
    sweep(one, two, force_ref, tiles, lane_ids, coarse)
    sweep(two, one, force_ref, tiles, lane_ids)

    def pair(_, carry):
        sweep(one, two, force_ref, tiles, lane_ids)
        sweep(two, one, force_ref, tiles, lane_ids)
        return carry

    lax.fori_loop(0, STEPS // 2 - 1, pair, 0)
    first = jnp.where(slab == 0, 0.0, 1.0)
    for i in range(1, count - 1):
        rows = pl.ds(PAD + 8 * i, 8)
        for g in range(TILES):
            fine = one[g, rows, :]
            rough = coarse[g, rows, :]
            gift_ref[g, rows, :] = fine - first * rough
            defect_ref[pl.ds(8 * i, 8), pl.ds(g * LANE, LANE)] = fine - rough


def far_kernel(raw_ref, force_ref, far_ref, one, two, force, coarse):
    slab = lax.axis_index("tm")
    lane_ids = lanes()
    count = FAR_BOX // 8
    tiles = [PAD + 8 * i for i in range(count)]
    load(one, PAD, raw_ref, 0, count, ADVECT)
    low = pl.multiple_of(PAD + FAR_BOX // 2 * inner_place(slab), 8)
    for g in range(TILES):
        for i in range(count):
            force[g, pl.ds(PAD + 8 * i, 8), :] = force_ref[g, pl.ds(low + 8 * i, 8), :]
    sweep(one, two, force, tiles, lane_ids, coarse)
    sweep(two, one, force, tiles, lane_ids)

    def pair(_, carry):
        sweep(one, two, force, tiles, lane_ids)
        sweep(two, one, force, tiles, lane_ids)
        return carry

    lax.fori_loop(0, STEPS // 2 - 1, pair, 0)
    first = jnp.where(slab ^ 2 == 0, 0.0, 1.0)
    start = PAD + REACH + (PART - FAR_BOX // 2) * inner_place(slab)
    for i in range(BLOCK // 8):
        rows = pl.ds(start + 8 * i, 8)
        for g in range(TILES):
            far_ref[pl.ds(8 * i, 8), pl.ds(g * LANE, LANE)] = one[g, rows, :] - first * coarse[g, rows, :]


def rim_kernel(c_ref, s_ref, intra_ref, inter_ref, inner_gift_ref, inner_force_ref, defect_ref, mine_ref, one_ref, two_ref, block_ref, rim_gift_ref, wide_force, one, two, force, coarse, gift):
    slab, odd, up_mask, down_mask = place()
    lane_ids = lanes()
    low, high = PAD, SIDE + PAD
    third = HALO // 8

    def fill(target, scale, top, main, bottom, offset):
        load(target, low, top, offset, third, scale * up_mask)
        load(target, low + HALO, main, 0, third, scale)
        load(target, high, main, ROWS - HALO, third, scale)
        load(target, high + HALO, bottom, offset, third, scale * down_mask)

    @pl.when(odd == 1)
    def _():
        fill(one, ADVECT, intra_ref, c_ref, inter_ref, 0)
        fill(force, ADVECT * FORCE, intra_ref, s_ref, inter_ref, HALO)

    @pl.when(odd == 0)
    def _():
        fill(one, ADVECT, inter_ref, c_ref, intra_ref, 0)
        fill(force, ADVECT * FORCE, inter_ref, s_ref, intra_ref, HALO)

    def tiles(first, last):
        upper = [low + 8 * i for i in range(first, last)]
        lower = [high + 8 * i for i in range(2 * third - last, 2 * third - first)]
        return upper + lower

    masks = {low + 8 * i: up_mask for i in range(third)}
    masks.update({high + HALO + 8 * i: down_mask for i in range(third)})
    sweep(one, two, force, tiles(0, 6), lane_ids, coarse, masks)
    sweep(two, one, force, tiles(1, 6), lane_ids, None, masks)
    sweep(one, two, force, tiles(1, 6), lane_ids, None, masks)
    sweep(two, one, force, tiles(1, 5), lane_ids, None, masks)

    def pair(_, carry):
        sweep(one, two, force, tiles(1, 5), lane_ids, None, masks)
        sweep(two, one, force, tiles(1, 5), lane_ids, None, masks)
        return carry

    lax.fori_loop(0, STEPS // 2 - 2, pair, 0)
    first = jnp.where(slab == 0, 0.0, 1.0)
    base = 2 * REACH
    for g in range(TILES):
        for i in range(1, ROWS // 8 - 1):
            gift[g, pl.ds(base + 8 * i, 8), :] = inner_gift_ref[g, pl.ds(PAD + 8 * i, 8), :]
        for i in range(ROWS // 8):
            wide_force[g, pl.ds(base + 8 * i, 8), :] = inner_force_ref[g, pl.ds(PAD + 8 * i, 8), :]
        for i in range(2):
            wide_force[g, pl.ds(8 * i, 8), :] = force[g, pl.ds(low + 8 + 8 * i, 8), :]
            wide_force[g, pl.ds(base + ROWS + 8 * i, 8), :] = force[g, pl.ds(high + HALO + 8 * i, 8), :]
    for n, at in enumerate([low + 8, low + 16, low + 24, high + 16, high + 24, high + 32]):
        rows = pl.ds(at, 8)
        place_at = 8 * n if n < 3 else base + ROWS - 8 + 8 * (n - 3)
        for g in range(TILES):
            fine = one[g, rows, :]
            rough = coarse[g, rows, :]
            if at in masks:
                rough = rough * masks[at]
            given = fine - first * rough
            gift[g, pl.ds(place_at, 8), :] = given
            if at in (low + HALO, high + HALO - 8):
                cut = (pl.ds(0 if at == low + HALO else 8, 8), pl.ds(g * LANE, LANE))
                defect_ref[cut] = fine - rough
                rim_gift_ref[cut] = given
    for order, out in ((0, mine_ref), (2, one_ref), (3, two_ref)):
        worker = slab ^ partner(order)

        def cut(out, source, starts):
            for i in range(BOX // 8):
                at = starts[0] + 8 * i if i < PIECE // 8 else starts[1] + 8 * i - PIECE
                for g in range(TILES):
                    piece = source[g, pl.ds(at, 8), :]
                    if len(out.shape) == 3:
                        out[g, pl.ds(8 * i, 8), :] = piece
                    else:
                        out[pl.ds(8 * i, 8), pl.ds(g * LANE, LANE)] = piece

        def cut_all(starts, order=order, out=out):
            cut(out, gift, starts)
            if order == 0:
                cut(block_ref, wide_force, starts)

        @pl.when(worker == RIM_SLAB)
        def _(cut_all=cut_all):
            cut_all((base - FAR, base + ROWS + FAR - PIECE))

        @pl.when(worker != RIM_SLAB)
        def _(cut_all=cut_all, worker=worker):
            start = base + inner_start(worker)
            cut_all((start, start + PIECE))


def each_place(slab, odd, body):
    for t in range(SLABS):
        for core in range(2):
            pl.when((slab == t) & (odd == core))(functools.partial(body, t, ORDERS[core]))


def chain_kernel(mine_ref, one_ref, two_ref, three_ref, force_ref, out0_ref, out1_ref, out2_ref, out3_ref, start1, start2, start3):
    slab, odd, up_mask, down_mask = place()
    lane_ids = lanes()
    boxes = (mine_ref, one_ref, two_ref, three_ref)
    outs = (out0_ref, out1_ref, out2_ref, out3_ref)
    row_ids = lax.broadcasted_iota(jnp.int32, (8, LANE), 0)
    masks = {
        0: up_mask,
        1: jnp.where(row_ids < FAR - 8, up_mask, 1.0),
        4: jnp.where(row_ids >= 8 - (FAR - 8), down_mask, 1.0),
        5: down_mask,
    }

    def leap(source, target, defect, rim):
        for i in range((BOX if rim else BLOCK) // 8):
            at = PAD + 8 * i
            for g, now, above, below, left, right in row_tile(source, at, lane_ids):
                inc = increment(now, above, below, left, right, force_ref[g, pl.ds(8 * i, 8), :])
                new = now + 8.0 * inc + defect[pl.ds(8 * i, 8), pl.ds(g * LANE, LANE)]
                target[g, pl.ds(at, 8), :] = new * masks[i] if rim and i in masks else new

    def body(t, order):
        rim = t == RIM_SLAB
        load(start1, PAD, boxes[order.index(t)], 0, (BOX if rim else BLOCK) // 8, 1.0)
        leap(start1, start2, boxes[order.index(t ^ 1)], rim)
        leap(start2, start3, boxes[order.index(t ^ 2)], rim)
        starts = (None, start1, start2, start3)
        pieces = ((0, 2, EDGE), (EDGE, BOX - 2 - EDGE, EDGE)) if rim else ((0, 2, PART),)
        for k in range(SLABS):
            begin = starts[max(t ^ order[k], 1)]
            for to, at, rows in pieces:
                for i in range((rows + 7) // 8):
                    size = min(8, rows - 8 * i)
                    for g in range(TILES):
                        outs[k][pl.ds(to + 8 * i, size), pl.ds(g * LANE, LANE)] = begin[g, pl.ds(PAD + at + 8 * i, size), :]

    each_place(slab, odd, body)


def first_kernel(inner_gift_ref, rim_gift_ref, new_out, end_out, stage, sems):
    @pl.when(lax.axis_index("tm") == 0)
    def _():
        last = ROWS // 8 - 1
        for g in range(TILES):
            cut = pl.ds(g * LANE, LANE)
            for i in range(last + 1):
                if i in (0, last):
                    value = rim_gift_ref[pl.ds(8 * (i > 0), 8), cut]
                else:
                    value = inner_gift_ref[g, pl.ds(PAD + 8 * i, 8), :]
                stage[pl.ds(8 * i, 8), cut] = value * (1.0 / ADVECT)
        copies = [pltpu.make_async_copy(stage, out, sems.at[n]) for n, out in enumerate((new_out, end_out))]
        for copy in copies:
            copy.start()
        for copy in copies:
            copy.wait()


def fine_kernel(*refs):
    pl.when(lax.axis_index("tm") > 0)(functools.partial(later_slabs, *refs))


def later_slabs(defect_ref, rim_defect_ref, force, mine_ref, one_ref, two_ref, three_ref, new_in, end_in, new_out, end_out, one, two, new_ref, end_ref, sems):
    boxes = (mine_ref, one_ref, two_ref, three_ref)
    slab, odd, up_mask, down_mask = place()
    lane_ids = lanes()
    base = PAD + REACH
    last = base + ROWS

    def body(t, order):
        for w in range(SLABS):
            source = boxes[order.index(t ^ w)]
            if w == RIM_SLAB:
                pieces = ((0, -REACH, EDGE), (EDGE, ROWS + REACH - EDGE, EDGE))
            else:
                pieces = ((0, EDGE - REACH + PART * (w - (w > RIM_SLAB)), PART),)
            for begin, row, rows in pieces:
                for i in range((rows + 7) // 8):
                    size = min(8, rows - 8 * i)
                    for g in range(TILES):
                        one[g, pl.ds(base + row + 8 * i, size), :] = source[pl.ds(begin + 8 * i, size), pl.ds(g * LANE, LANE)]

    each_place(slab, odd, body)

    tiles = [PAD + 8 * i for i in range((ROWS + 2 * REACH) // 8)]
    masks = {PAD: up_mask, last: down_mask}
    for at in tiles:
        for g, now, above, below, left, right in row_tile(one, at, lane_ids):
            inc = increment(now, above, below, left, right, force[g, pl.ds(at, 8), :])
            new = now + inc
            cut = pl.ds(g * LANE, LANE)
            if at in masks:
                new = new * masks[at]
            else:
                if at == base:
                    defect = rim_defect_ref[pl.ds(0, 8), cut]
                elif at == last - 8:
                    defect = rim_defect_ref[pl.ds(8, 8), cut]
                else:
                    defect = defect_ref[pl.ds(at - base, 8), cut]
                new_ref[pl.ds(at - base, 8), cut] = (now + 8.0 * inc + defect) * (1.0 / ADVECT)
            two[g, pl.ds(at, 8), :] = new

    copies = [pltpu.make_async_copy(new_ref, new_out, sems.at[0])]
    copies[0].start()

    def pair(_, carry):
        sweep(two, one, force, tiles, lane_ids, None, masks)
        sweep(one, two, force, tiles, lane_ids, None, masks)
        return carry

    lax.fori_loop(0, STEPS // 2 - 1, pair, 0)
    for at in tiles[1:-1]:
        for g, now, above, below, left, right in row_tile(two, at, lane_ids):
            inc = increment(now, above, below, left, right, force[g, pl.ds(at, 8), :])
            end_ref[pl.ds(at - base, 8), pl.ds(g * LANE, LANE)] = (now + inc) * (1.0 / ADVECT)
        done = at + 8 - base
        if done % CHUNK == 0:
            rows = pl.ds(done - CHUNK, CHUNK)
            copies.append(pltpu.make_async_copy(end_ref.at[rows], end_out.at[rows], sems.at[len(copies)]))
            copies[-1].start()
    for copy in copies:
        copy.wait()


def swap(array, axis, by):
    size = lax.axis_size(axis)
    return lax.ppermute(array, axis, [(i, i ^ by) for i in range(size)])


def swap_one(box, order):
    count, width = lax.axis_size("tm"), lax.axis_size("space")
    pairs = []
    for t in range(count):
        for strip in range(width):
            by = ORDERS[strip % 2][order]
            pairs.append((t * width + strip, (t ^ by) * width + strip))
    return lax.ppermute(box, ("tm", "space"), pairs)


def call(kernel, outs, scratch, place=pltpu.VMEM, copies=0, **more):
    spec = pl.BlockSpec(memory_space=place)
    return pl.pallas_call(
        kernel,
        out_shape=[jax.ShapeDtypeStruct(shape, jnp.float32) for shape in outs],
        out_specs=[spec] * len(outs),
        scratch_shapes=[pltpu.VMEM(shape, jnp.float32) for shape in scratch]
        + [pltpu.SemaphoreType.DMA((copies,))] * (copies > 0),
        compiler_params=pltpu.CompilerParams(vmem_limit_bytes=24 * 1024 * 1024),
        **more,
    )


def local(c_points, source):
    field = c_points[0]
    count = lax.axis_size("space")
    edges = jax.ShapeDtypeStruct((2 * HALO, COLS), jnp.float32)
    to_intra, to_inter, to_far = pl.pallas_call(
        pack_kernel,
        out_shape=[edges, edges, jax.ShapeDtypeStruct((FAR_BOX, COLS), jnp.float32)],
        in_specs=[pl.BlockSpec(memory_space=pl.ANY)] * 2,
        out_specs=[pl.BlockSpec(memory_space=pltpu.VMEM)] * 3,
        scratch_shapes=[pltpu.SemaphoreType.DMA((5,))],
    )(c_points, source)
    pairs = []
    for t in range(lax.axis_size("tm")):
        for strip in range(count):
            if strip in (0, count - 1):
                mate = (t ^ 1) * count + strip
            else:
                mate = t * count + strip + (1 if strip % 2 else -1)
            pairs.append((t * count + strip, mate))
    inter = lax.ppermute(to_inter, ("tm", "space"), pairs)
    intra = swap(to_intra, "space", 1)

    wide = (TILES, ROWS + 2 * PAD, LANE)
    raw = swap_one(to_far, 1)
    defect, gift, force = call(inner_kernel, [(ROWS, COLS), wide, wide], [wide] * 3)(field, source)
    narrow = (TILES, ROWS + 4 * REACH, LANE)
    rim_defect, mine, one, two, block_force, rim_gift, wide_force = call(
        rim_kernel,
        [(16, COLS)] + [(BOX, COLS)] * 3 + [(TILES, BOX, LANE), (16, COLS), narrow],
        [(TILES, 2 * SIDE, LANE)] * 4 + [narrow],
    )(field, source, intra, inter, gift, force)
    one, two = swap_one(one, 2), swap_one(two, 3)
    far = call(far_kernel, [(BLOCK, COLS)], [(TILES, FAR_BOX + 2 * PAD, LANE)] * 4)(raw, force)[0]
    starts = call(
        chain_kernel, [(PART, COLS)] * 4, [(TILES, BOX + 2 * PAD, LANE)] * 3
    )(mine, far, one, two, block_force)
    starts = [starts[0]] + [swap_one(starts[order], order) for order in range(1, SLABS)]
    new, end = call(first_kernel, [(ROWS, COLS)] * 2, [(ROWS, COLS)], pl.ANY, 2)(gift, rim_gift)
    middle = (TILES, ROWS + 2 * REACH + 2 * PAD, LANE)
    inside, outside = pl.BlockSpec(memory_space=pltpu.VMEM), pl.BlockSpec(memory_space=pl.ANY)
    corrected, fine = call(
        fine_kernel,
        [(ROWS, COLS)] * 2,
        [middle] * 2 + [(ROWS, COLS)] * 2,
        pl.ANY,
        1 + ROWS // CHUNK,
        in_specs=[inside] * 7 + [outside] * 2,
        input_output_aliases={7: 0, 8: 1},
    )(defect, rim_defect, wide_force, *starts, new, end)
    return corrected[None], fine[None]


def solution(mesh):
    return jax.shard_map(
        local,
        mesh=mesh,
        in_specs=(P("tm", "space", None), P("space", None)),
        out_specs=(P("tm", "space", None), P("tm", "space", None)),
        check_vma=False,
    )
```

```python
import functools

import jax
import jax.numpy as jnp
from jax import lax
from jax.experimental import pallas as pl
from jax.experimental.pallas import tpu as pltpu
from jax.sharding import PartitionSpec as P

ADVECT = 0.02
DIFFUSE = 0.01
FORCE = 0.05
STEPS = 8
SLABS = 4
ROWS = 128
COLS = 1024
LANE = 128
TILES = COLS // LANE
HALO = 24
DEEP = 18
PAD = 8
REACH = STEPS
PART = (ROWS + 2 * REACH) // SLABS
BLOCK = PART + 4
BOX = 44
FAR_BOX = BLOCK + 2 * REACH
CHUNK = 32
PIECE = BOX // 2
BOX_TILES = (0, 8, 16, 24, 32, BOX - 8)
EDGE = PART // 2
FAR = REACH + 2
RIM_SLAB = 1
RIM = 2 * HALO
SIDE = RIM + 2 * PAD


ORDERS = ((0, 2, 1, 3), (0, 2, 3, 1))


def increment(now, above, below, left, right, force):
    twice = now + now
    rear = above + left - twice
    ahead = below + right - twice
    gain = jnp.maximum(now, 0.0) + DIFFUSE
    return force + gain * rear + (gain - now) * ahead


def row_tile(state, start, lane_ids):
    now = [state[g, pl.ds(start, 8), :] for g in range(TILES)]
    above = [state[g, pl.ds(start - 1, 8), :] for g in range(TILES)]
    below = [state[g, pl.ds(start + 1, 8), :] for g in range(TILES)]
    for g in range(TILES):
        left = pltpu.roll(jnp.where(lane_ids == LANE - 1, now[g - 1], now[g]), 1, 1)
        right = pltpu.roll(jnp.where(lane_ids == 0, now[(g + 1) % TILES], now[g]), LANE - 1, 1)
        yield g, now[g], above[g], below[g], left, right


def lanes():
    return lax.broadcasted_iota(jnp.int32, (8, LANE), 1)


def parity():
    return lax.axis_index("space") % 2


def place():
    slab = lax.axis_index("tm")
    strip = lax.axis_index("space")
    up_mask = jnp.where(strip == 0, 0.0, 1.0)
    down_mask = jnp.where(strip == lax.axis_size("space") - 1, 0.0, 1.0)
    return slab, strip % 2, up_mask, down_mask


def pack_kernel(c_ref, s_ref, inter_ref, far_ref, intra_ref):
    odd = parity()

    def edges(core):
        top, bottom = 0, ROWS - DEEP
        for out, start in ((inter_ref, bottom if core else top), (intra_ref, top if core else bottom)):
            for n, source in enumerate((c_ref, s_ref)):
                for i in range(0, DEEP, 8):
                    size = min(8, DEEP - i)
                    for g in range(TILES):
                        piece = source[pl.ds(start + i, size), pl.ds(g * LANE, LANE)]
                        out[pl.ds(2 * DEEP * g + DEEP * n + i, size), :] = piece

    def inner(place):
        for i in range(0, FAR_BOX, 8):
            far_ref[pl.ds(i, 8), :] = c_ref[pl.ds(PART * place + i, 8), :]

    for core in range(2):
        pl.when(odd == core)(functools.partial(edges, core))
    wanted = inner_place(lax.axis_index("tm") ^ 2)
    for place in range(SLABS - 1):
        pl.when(wanted == place)(functools.partial(inner, place))


def load_deep(target, at, source, begin, scale):
    for i in range(0, DEEP, 8):
        size = min(8, DEEP - i)
        for g in range(TILES):
            target[g, pl.ds(at + i, size), :] = source[pl.ds(2 * DEEP * g + begin + i, size), :] * scale


def load(target, at, source, start, count, scale):
    for i in range(count):
        for g in range(TILES):
            target[g, pl.ds(at + 8 * i, 8), :] = source[pl.ds(start + 8 * i, 8), pl.ds(g * LANE, LANE)] * scale


def sweep(source, target, force, tiles, lane_ids, coarse=None, masks=None):
    for at in tiles:
        for g, now, above, below, left, right in row_tile(source, at, lane_ids):
            inc = increment(now, above, below, left, right, force[g, pl.ds(at, 8), :])
            new = now + inc
            if coarse is not None:
                coarse[g, pl.ds(at, 8), :] = now + 8.0 * inc
            if masks and at in masks:
                new = new * masks[at]
            target[g, pl.ds(at, 8), :] = new


def partner(place):
    first, second = ORDERS[0][place], ORDERS[1][place]
    return first if first == second else jnp.where(parity() == 0, first, second)


def inner_place(worker):
    return jnp.where(worker > RIM_SLAB, worker - 1, 0)


def inner_start(worker):
    return REACH + PART * inner_place(worker)


def inner_kernel(c_ref, s_ref, defect_ref, gift_ref, force_ref, one, two, coarse):
    slab = lax.axis_index("tm")
    lane_ids = lanes()
    count = ROWS // 8
    load(one, PAD, c_ref, 0, count, ADVECT)
    load(force_ref, PAD, s_ref, 0, count, ADVECT * FORCE)
    tiles = [PAD + 8 * i for i in range(count)]
    sweep(one, two, force_ref, tiles, lane_ids, coarse)
    sweep(two, one, force_ref, tiles, lane_ids)

    def pair(_, carry):
        sweep(one, two, force_ref, tiles, lane_ids)
        sweep(two, one, force_ref, tiles, lane_ids)
        return carry

    lax.fori_loop(0, STEPS // 2 - 1, pair, 0)
    first = jnp.where(slab == 0, 0.0, 1.0)
    for i in range(1, count - 1):
        rows = pl.ds(PAD + 8 * i, 8)
        for g in range(TILES):
            fine = one[g, rows, :]
            rough = coarse[g, rows, :]
            gift_ref[g, rows, :] = fine - first * rough
            defect_ref[pl.ds(8 * i, 8), pl.ds(g * LANE, LANE)] = fine - rough


def far_kernel(raw_ref, force_ref, far_ref, one, two, force, coarse):
    slab = lax.axis_index("tm")
    lane_ids = lanes()
    count = FAR_BOX // 8
    tiles = [PAD + 8 * i for i in range(count)]
    load(one, PAD, raw_ref, 0, count, ADVECT)
    low = PAD + PART * inner_place(slab)
    for g in range(TILES):
        for i in range(count):
            force[g, pl.ds(PAD + 8 * i, 8), :] = force_ref[g, pl.ds(low + 8 * i, 8), :]
    sweep(one, two, force, tiles, lane_ids, coarse)
    sweep(two, one, force, tiles, lane_ids)

    def pair(_, carry):
        sweep(one, two, force, tiles, lane_ids)
        sweep(two, one, force, tiles, lane_ids)
        return carry

    lax.fori_loop(0, STEPS // 2 - 1, pair, 0)
    first = jnp.where(slab ^ 2 == 0, 0.0, 1.0)
    start = PAD + REACH
    for i in range(BLOCK // 8):
        rows = pl.ds(start + 8 * i, 8)
        for g in range(TILES):
            far_ref[pl.ds(8 * i, 8), pl.ds(g * LANE, LANE)] = one[g, rows, :] - first * coarse[g, rows, :]


def rim_kernel(c_ref, s_ref, intra_ref, inter_ref, inner_gift_ref, inner_force_ref, defect_ref, mine_ref, one_ref, two_ref, block_ref, rim_gift_ref, rim_force_ref, one, two, force, coarse):
    slab, odd, up_mask, down_mask = place()
    lane_ids = lanes()
    low, high = PAD, SIDE + PAD
    third = HALO // 8

    def fill(target, scale, top, main, bottom, offset):
        load_deep(target, low + HALO - DEEP, top, offset, scale * up_mask)
        load(target, low + HALO, main, 0, third, scale)
        load(target, high, main, ROWS - HALO, third, scale)
        load_deep(target, high + HALO, bottom, offset, scale * down_mask)

    @pl.when(odd == 1)
    def _():
        fill(one, ADVECT, intra_ref, c_ref, inter_ref, 0)
        fill(force, ADVECT * FORCE, intra_ref, s_ref, inter_ref, DEEP)

    @pl.when(odd == 0)
    def _():
        fill(one, ADVECT, inter_ref, c_ref, intra_ref, 0)
        fill(force, ADVECT * FORCE, inter_ref, s_ref, intra_ref, DEEP)

    def tiles(first, last):
        upper = [low + 8 * i for i in range(first, last)]
        lower = [high + 8 * i for i in range(2 * third - last, 2 * third - first)]
        return upper + lower

    masks = {low + 8 * i: up_mask for i in range(third)}
    masks.update({high + HALO + 8 * i: down_mask for i in range(third)})
    sweep(one, two, force, tiles(0, 6), lane_ids, coarse, masks)
    sweep(two, one, force, tiles(1, 6), lane_ids, None, masks)
    sweep(one, two, force, tiles(1, 6), lane_ids, None, masks)
    sweep(two, one, force, tiles(1, 5), lane_ids, None, masks)

    def pair(_, carry):
        sweep(one, two, force, tiles(1, 5), lane_ids, None, masks)
        sweep(two, one, force, tiles(1, 5), lane_ids, None, masks)
        return carry

    lax.fori_loop(0, STEPS // 2 - 2, pair, 0)
    first = jnp.where(slab == 0, 0.0, 1.0)
    for at in tiles(1, 5):
        rows = pl.ds(at, 8)
        for g in range(TILES):
            fine = one[g, rows, :]
            rough = coarse[g, rows, :]
            if at in masks:
                rough = rough * masks[at]
            given = fine - first * rough
            two[g, rows, :] = given
            if at in (low + HALO, high + HALO - 8):
                cut = (pl.ds(0 if at == low + HALO else 8, 8), pl.ds(g * LANE, LANE))
                defect_ref[cut] = fine - rough
                rim_gift_ref[cut] = given
    for g in range(TILES):
        for i in range(2):
            rim_force_ref[g, pl.ds(8 * i, 8), :] = force[g, pl.ds(low + 8 + 8 * i, 8), :]
            rim_force_ref[g, pl.ds(16 + 8 * i, 8), :] = force[g, pl.ds(high + HALO + 8 * i, 8), :]
    ends = (low + HALO - FAR, high + HALO + FAR - PIECE)
    for order, out in ((0, mine_ref), (2, one_ref), (3, two_ref)):
        worker = slab ^ partner(order)

        def cut_rim(order=order, out=out):
            for n, start in enumerate(ends):
                for i in range(0, PIECE, 8):
                    size = min(8, PIECE - i)
                    for g in range(TILES):
                        rows = pl.ds(start + i, size)
                        out[pl.ds(BOX * g + PIECE * n + i, size), :] = two[g, rows, :]
                        if order == 0:
                            block_ref[g, pl.ds(PIECE * n + i, size), :] = force[g, rows, :]

        def cut_inner(order=order, out=out, worker=worker):
            start = PAD + inner_start(worker)
            for i in range(0, BLOCK, 8):
                for g in range(TILES):
                    rows = pl.ds(start + i, 8)
                    out[pl.ds(BOX * g + i, 8), :] = inner_gift_ref[g, rows, :]
                    if order == 0:
                        block_ref[g, pl.ds(i, 8), :] = inner_force_ref[g, rows, :]

        pl.when(worker == RIM_SLAB)(cut_rim)
        pl.when(worker != RIM_SLAB)(cut_inner)


def each_place(slab, odd, body):
    for t in range(SLABS):
        for core in range(2):
            pl.when((slab == t) & (odd == core))(functools.partial(body, t, ORDERS[core]))


def chain_kernel(mine_ref, one_ref, two_ref, three_ref, force_ref, out0_ref, out1_ref, out2_ref, out3_ref, start1, start2, start3):
    slab, odd, up_mask, down_mask = place()
    lane_ids = lanes()
    boxes = (mine_ref, one_ref, two_ref, three_ref)
    outs = (out0_ref, out1_ref, out2_ref, out3_ref)
    row_ids = lax.broadcasted_iota(jnp.int32, (8, LANE), 0)
    def mask_at(at):
        row = row_ids + at
        row = jnp.where(row < PIECE, row - FAR, row + (ROWS + FAR - BOX))
        return jnp.where(row < 0, up_mask, jnp.where(row >= ROWS, down_mask, 1.0))

    masks = {at: mask_at(at) for at in (0, 8, 32, BOX - 8)}

    def read(box, at, g):
        if box.shape[1] == COLS:
            return box[pl.ds(at, 8), pl.ds(g * LANE, LANE)]
        return box[pl.ds(BOX * g + at, 8), :]

    def leap(source, target, defect, tiles, rim):
        for at in tiles:
            for g, now, above, below, left, right in row_tile(source, PAD + at, lane_ids):
                inc = increment(now, above, below, left, right, force_ref[g, pl.ds(at, 8), :])
                new = now + 8.0 * inc + read(defect, at, g)
                target[g, pl.ds(PAD + at, 8), :] = new * masks[at] if rim and at in masks else new

    def body(t, order):
        rim = t == RIM_SLAB
        tiles = BOX_TILES if rim else BOX_TILES[: BLOCK // 8]
        for at in tiles:
            for g in range(TILES):
                start1[g, pl.ds(PAD + at, 8), :] = read(boxes[order.index(t)], at, g)
        leap(start1, start2, boxes[order.index(t ^ 1)], tiles, rim)
        leap(start2, start3, boxes[order.index(t ^ 2)], tiles, rim)
        starts = (None, start1, start2, start3)
        pieces = ((0, 2, EDGE), (EDGE, PIECE + 2, EDGE)) if rim else ((0, 2, PART),)
        for k in range(SLABS):
            begin = starts[max(t ^ order[k], 1)]
            for to, at, rows in pieces:
                for i in range(0, rows, 8):
                    size = min(8, rows - i)
                    for g in range(TILES):
                        outs[k][pl.ds(PART * g + to + i, size), :] = begin[g, pl.ds(PAD + at + i, size), :]

    each_place(slab, odd, body)


def first_kernel(inner_gift_ref, rim_gift_ref, inner_force_ref, rim_force_ref, new_out, end_out, wide_force, stage, sems):
    for g in range(TILES):
        for i in range(2):
            wide_force[g, pl.ds(8 * i, 8), :] = rim_force_ref[g, pl.ds(8 * i, 8), :]
            wide_force[g, pl.ds(16 + ROWS + 8 * i, 8), :] = rim_force_ref[g, pl.ds(16 + 8 * i, 8), :]
        for i in range(ROWS // 8):
            wide_force[g, pl.ds(16 + 8 * i, 8), :] = inner_force_ref[g, pl.ds(PAD + 8 * i, 8), :]

    @pl.when(lax.axis_index("tm") == 0)
    def _():
        last = ROWS // 8 - 1
        for g in range(TILES):
            cut = pl.ds(g * LANE, LANE)
            for i in range(last + 1):
                if i in (0, last):
                    value = rim_gift_ref[pl.ds(8 * (i > 0), 8), cut]
                else:
                    value = inner_gift_ref[g, pl.ds(PAD + 8 * i, 8), :]
                stage[pl.ds(8 * i, 8), cut] = value * (1.0 / ADVECT)
        copies = [pltpu.make_async_copy(stage, out, sems.at[n]) for n, out in enumerate((new_out, end_out))]
        for copy in copies:
            copy.start()
        for copy in copies:
            copy.wait()


def fine_kernel(*refs):
    pl.when(lax.axis_index("tm") > 0)(functools.partial(later_slabs, *refs))


def later_slabs(defect_ref, rim_defect_ref, force, mine_ref, one_ref, two_ref, three_ref, new_in, end_in, new_out, end_out, one, two, new_ref, end_ref, sems):
    boxes = (mine_ref, one_ref, two_ref, three_ref)
    slab, odd, up_mask, down_mask = place()
    lane_ids = lanes()
    base = PAD + REACH
    last = base + ROWS

    def body(t, order):
        for w in range(SLABS):
            source = boxes[order.index(t ^ w)]
            if w == RIM_SLAB:
                pieces = ((0, -REACH, EDGE), (EDGE, ROWS + REACH - EDGE, EDGE))
            else:
                pieces = ((0, EDGE - REACH + PART * (w - (w > RIM_SLAB)), PART),)
            for begin, row, rows in pieces:
                for i in range(0, rows, 8):
                    size = min(8, rows - i)
                    for g in range(TILES):
                        one[g, pl.ds(base + row + i, size), :] = source[pl.ds(PART * g + begin + i, size), :]

    each_place(slab, odd, body)

    tiles = [PAD + 8 * i for i in range((ROWS + 2 * REACH) // 8)]
    masks = {PAD: up_mask, last: down_mask}
    for at in tiles:
        for g, now, above, below, left, right in row_tile(one, at, lane_ids):
            inc = increment(now, above, below, left, right, force[g, pl.ds(at, 8), :])
            new = now + inc
            cut = pl.ds(g * LANE, LANE)
            if at in masks:
                new = new * masks[at]
            else:
                if at == base:
                    defect = rim_defect_ref[pl.ds(0, 8), cut]
                elif at == last - 8:
                    defect = rim_defect_ref[pl.ds(8, 8), cut]
                else:
                    defect = defect_ref[pl.ds(at - base, 8), cut]
                new_ref[pl.ds(at - base, 8), cut] = (now + 8.0 * inc + defect) * (1.0 / ADVECT)
            two[g, pl.ds(at, 8), :] = new

    copies = [pltpu.make_async_copy(new_ref, new_out, sems.at[0])]
    copies[0].start()

    def pair(_, carry):
        sweep(two, one, force, tiles, lane_ids, None, masks)
        sweep(one, two, force, tiles, lane_ids, None, masks)
        return carry

    lax.fori_loop(0, STEPS // 2 - 1, pair, 0)
    for at in tiles[1:-1]:
        for g, now, above, below, left, right in row_tile(two, at, lane_ids):
            inc = increment(now, above, below, left, right, force[g, pl.ds(at, 8), :])
            end_ref[pl.ds(at - base, 8), pl.ds(g * LANE, LANE)] = (now + inc) * (1.0 / ADVECT)
        done = at + 8 - base
        if done % CHUNK == 0:
            rows = pl.ds(done - CHUNK, CHUNK)
            copies.append(pltpu.make_async_copy(end_ref.at[rows], end_out.at[rows], sems.at[len(copies)]))
            copies[-1].start()
    for copy in copies:
        copy.wait()


def swap(array, axis, by):
    size = lax.axis_size(axis)
    return lax.ppermute(array, axis, [(i, i ^ by) for i in range(size)])


def swap_one(box, order):
    count, width = lax.axis_size("tm"), lax.axis_size("space")
    pairs = []
    for t in range(count):
        for strip in range(width):
            by = ORDERS[strip % 2][order]
            pairs.append((t * width + strip, (t ^ by) * width + strip))
    return lax.ppermute(box, ("tm", "space"), pairs)


def call(kernel, outs, scratch, place=pltpu.VMEM, copies=0, **more):
    places = place if isinstance(place, list) else [place] * len(outs)
    return pl.pallas_call(
        kernel,
        out_shape=[jax.ShapeDtypeStruct(shape, jnp.float32) for shape in outs],
        out_specs=[pl.BlockSpec(memory_space=space) for space in places],
        scratch_shapes=[pltpu.VMEM(shape, jnp.float32) for shape in scratch]
        + [pltpu.SemaphoreType.DMA((copies,))] * (copies > 0),
        compiler_params=pltpu.CompilerParams(vmem_limit_bytes=24 * 1024 * 1024),
        **more,
    )


def local(c_points, source):
    count = lax.axis_size("space")
    edges = (TILES * 2 * DEEP, LANE)
    field = c_points[0]
    to_inter, to_far, to_intra = call(pack_kernel, [edges, (FAR_BOX, COLS), edges], [])(field, source)
    pairs = []
    for t in range(lax.axis_size("tm")):
        for strip in range(count):
            if strip in (0, count - 1):
                mate = (t ^ 1) * count + strip
            else:
                mate = t * count + strip + (1 if strip % 2 else -1)
            pairs.append((t * count + strip, mate))
    inter = lax.ppermute(to_inter, ("tm", "space"), pairs)
    intra = swap(to_intra, "space", 1)

    wide = (TILES, ROWS + 2 * PAD, LANE)
    raw = swap_one(to_far, 1)
    defect, gift, force = call(inner_kernel, [(ROWS, COLS), wide, wide], [wide] * 3)(field, source)
    narrow = (TILES, ROWS + 4 * REACH, LANE)
    box = (TILES * BOX, LANE)
    rim_defect, mine, one, two, block_force, rim_gift, rim_force = call(
        rim_kernel,
        [(16, COLS), box, box, box, (TILES, 48, LANE), (16, COLS), (TILES, 32, LANE)],
        [(TILES, 2 * SIDE, LANE)] * 4,
    )(field, source, intra, inter, gift, force)
    one, two = swap_one(one, 2), swap_one(two, 3)
    far = call(far_kernel, [(BLOCK, COLS)], [(TILES, FAR_BOX + 2 * PAD, LANE)] * 4)(raw, force)[0]
    starts = call(
        chain_kernel, [(TILES * PART, LANE)] * 4, [(TILES, 48 + 2 * PAD, LANE)] * 3
    )(mine, far, one, two, block_force)
    starts = [starts[0]] + [swap_one(starts[order], order) for order in range(1, SLABS)]
    new, end, wide_force = call(
        first_kernel,
        [(ROWS, COLS), (ROWS, COLS), narrow],
        [(ROWS, COLS)],
        [pl.ANY, pl.ANY, pltpu.VMEM],
        2,
    )(gift, rim_gift, force, rim_force)
    middle = (TILES, ROWS + 2 * REACH + 2 * PAD, LANE)
    inside, outside = pl.BlockSpec(memory_space=pltpu.VMEM), pl.BlockSpec(memory_space=pl.ANY)
    corrected, fine = call(
        fine_kernel,
        [(ROWS, COLS)] * 2,
        [middle] * 2 + [(ROWS, COLS)] * 2,
        pl.ANY,
        1 + ROWS // CHUNK,
        in_specs=[inside] * 7 + [outside] * 2,
        input_output_aliases={7: 0, 8: 1},
    )(defect, rim_defect, wide_force, *starts, new, end)
    return corrected[None], fine[None]


def solution(mesh):
    return jax.shard_map(
        local,
        mesh=mesh,
        in_specs=(P("tm", "space", None), P("space", None)),
        out_specs=(P("tm", "space", None), P("tm", "space", None)),
        check_vma=False,
    )
```

```python
import functools

import jax
import jax.numpy as jnp
from jax import lax
from jax.experimental import pallas as pl
from jax.experimental.pallas import tpu as pltpu
from jax.sharding import PartitionSpec as P

ADVECT = 0.02
DIFFUSE = 0.01
FORCE = 0.05
STEPS = 8
SLABS = 4
ROWS = 128
COLS = 1024
LANE = 128
TILES = COLS // LANE
HALO = 24
DEEP = 18
PAD = 8
REACH = STEPS
PART = (ROWS + 2 * REACH) // SLABS
BLOCK = PART + 4
BOX = 44
FAR_BOX = BLOCK + 2 * REACH
CHUNK = 32
PIECE = BOX // 2
BOX_TILES = (0, 8, 16, 24, 32, BOX - 8)
EDGE = PART // 2
FAR = REACH + 2
RIM_SLAB = 1
RIM = 2 * HALO
SIDE = RIM + 2 * PAD


ORDERS = ((0, 2, 1, 3), (0, 2, 3, 1))


def increment(now, above, below, left, right, force):
    twice = now + now
    rear = above + left - twice
    ahead = below + right - twice
    gain = jnp.maximum(now, 0.0) + DIFFUSE
    return force + gain * rear + (gain - now) * ahead


def row_tile(state, start, lane_ids):
    now = [state[g, pl.ds(start, 8), :] for g in range(TILES)]
    above = [state[g, pl.ds(start - 1, 8), :] for g in range(TILES)]
    below = [state[g, pl.ds(start + 1, 8), :] for g in range(TILES)]
    for g in range(TILES):
        left = pltpu.roll(jnp.where(lane_ids == LANE - 1, now[g - 1], now[g]), 1, 1)
        right = pltpu.roll(jnp.where(lane_ids == 0, now[(g + 1) % TILES], now[g]), LANE - 1, 1)
        yield g, now[g], above[g], below[g], left, right


def lanes():
    return lax.broadcasted_iota(jnp.int32, (8, LANE), 1)


def parity():
    return lax.axis_index("space") % 2


def place():
    slab = lax.axis_index("tm")
    strip = lax.axis_index("space")
    up_mask = jnp.where(strip == 0, 0.0, 1.0)
    down_mask = jnp.where(strip == lax.axis_size("space") - 1, 0.0, 1.0)
    return slab, strip % 2, up_mask, down_mask


def pack_kernel(c_ref, s_ref, inter_ref, far_ref, intra_ref):
    odd = parity()

    def edges(core):
        top, bottom = 0, ROWS - DEEP
        for out, start in ((inter_ref, bottom if core else top), (intra_ref, top if core else bottom)):
            for n, source in enumerate((c_ref, s_ref)):
                for i in range(0, DEEP, 8):
                    size = min(8, DEEP - i)
                    for g in range(TILES):
                        piece = source[pl.ds(start + i, size), pl.ds(g * LANE, LANE)]
                        out[pl.ds(2 * DEEP * g + DEEP * n + i, size), :] = piece

    def inner(place):
        for i in range(0, FAR_BOX, 8):
            far_ref[pl.ds(i, 8), :] = c_ref[pl.ds(PART * place + i, 8), :]

    for core in range(2):
        pl.when(odd == core)(functools.partial(edges, core))
    wanted = inner_place(lax.axis_index("tm") ^ 2)
    for place in range(SLABS - 1):
        pl.when(wanted == place)(functools.partial(inner, place))


def load_deep(target, at, source, begin, scale):
    for i in range(0, DEEP, 8):
        size = min(8, DEEP - i)
        for g in range(TILES):
            target[g, pl.ds(at + i, size), :] = source[pl.ds(2 * DEEP * g + begin + i, size), :] * scale


def load(target, at, source, start, count, scale):
    for i in range(count):
        for g in range(TILES):
            target[g, pl.ds(at + 8 * i, 8), :] = source[pl.ds(start + 8 * i, 8), pl.ds(g * LANE, LANE)] * scale


def sweep(source, target, force, tiles, lane_ids, coarse=None, masks=None):
    for at in tiles:
        for g, now, above, below, left, right in row_tile(source, at, lane_ids):
            inc = increment(now, above, below, left, right, force[g, pl.ds(at, 8), :])
            new = now + inc
            if coarse is not None:
                coarse[g, pl.ds(at, 8), :] = now + 8.0 * inc
            if masks and at in masks:
                new = new * masks[at]
            target[g, pl.ds(at, 8), :] = new


def partner(place):
    first, second = ORDERS[0][place], ORDERS[1][place]
    return first if first == second else jnp.where(parity() == 0, first, second)


def inner_place(worker):
    return jnp.where(worker > RIM_SLAB, worker - 1, 0)


def inner_start(worker):
    return REACH + PART * inner_place(worker)


def inner_kernel(c_ref, s_ref, defect_ref, gift_ref, force_ref, trace_ref, one, two, coarse):
    slab = lax.axis_index("tm")
    lane_ids = lanes()
    count = ROWS // 8
    load(one, PAD, c_ref, 0, count, ADVECT)
    load(force_ref, PAD, s_ref, 0, count, ADVECT * FORCE)
    tiles = [PAD + 8 * i for i in range(count)]

    def note(step, state):
        for n, row in enumerate((REACH, ROWS - 2 * REACH)):
            for g in range(TILES):
                trace_ref[step, n, g] = state[g, pl.ds(PAD + row, 8), :]

    sweep(one, two, force_ref, tiles, lane_ids, coarse)
    note(1, two)
    sweep(two, one, force_ref, tiles, lane_ids)
    note(2, one)

    def pair(i, carry):
        sweep(one, two, force_ref, tiles, lane_ids)
        note(3 + 2 * i, two)
        sweep(two, one, force_ref, tiles, lane_ids)
        note(4 + 2 * i, one)
        return carry

    lax.fori_loop(0, STEPS // 2 - 1, pair, 0)
    first = jnp.where(slab == 0, 0.0, 1.0)
    for i in range(1, count - 1):
        rows = pl.ds(PAD + 8 * i, 8)
        for g in range(TILES):
            fine = one[g, rows, :]
            rough = coarse[g, rows, :]
            gift_ref[g, rows, :] = fine - first * rough
            defect_ref[pl.ds(8 * i, 8), pl.ds(g * LANE, LANE)] = fine - rough


def far_kernel(raw_ref, force_ref, far_ref, one, two, force, coarse):
    slab = lax.axis_index("tm")
    lane_ids = lanes()
    count = FAR_BOX // 8
    tiles = [PAD + 8 * i for i in range(count)]
    load(one, PAD, raw_ref, 0, count, ADVECT)
    low = PAD + PART * inner_place(slab)
    for g in range(TILES):
        for i in range(count):
            force[g, pl.ds(PAD + 8 * i, 8), :] = force_ref[g, pl.ds(low + 8 * i, 8), :]
    sweep(one, two, force, tiles, lane_ids, coarse)
    sweep(two, one, force, tiles, lane_ids)

    def pair(_, carry):
        sweep(one, two, force, tiles, lane_ids)
        sweep(two, one, force, tiles, lane_ids)
        return carry

    lax.fori_loop(0, STEPS // 2 - 1, pair, 0)
    first = jnp.where(slab ^ 2 == 0, 0.0, 1.0)
    start = PAD + REACH
    for i in range(BLOCK // 8):
        rows = pl.ds(start + 8 * i, 8)
        for g in range(TILES):
            far_ref[pl.ds(8 * i, 8), pl.ds(g * LANE, LANE)] = one[g, rows, :] - first * coarse[g, rows, :]


def rim_kernel(c_ref, s_ref, intra_ref, inter_ref, inner_gift_ref, inner_force_ref, trace_ref, defect_ref, mine_ref, one_ref, two_ref, block_ref, rim_gift_ref, rim_force_ref, one, two, force, coarse):
    slab, odd, up_mask, down_mask = place()
    lane_ids = lanes()
    low, high = PAD, SIDE + PAD
    third = HALO // 8

    def fill(target, scale, top, main, bottom, offset):
        load_deep(target, low + HALO - DEEP, top, offset, scale * up_mask)
        load(target, low + HALO, main, 0, third, scale)
        load(target, high, main, ROWS - HALO, third, scale)
        load_deep(target, high + HALO, bottom, offset, scale * down_mask)

    @pl.when(odd == 1)
    def _():
        fill(one, ADVECT, intra_ref, c_ref, inter_ref, 0)
        fill(force, ADVECT * FORCE, intra_ref, s_ref, inter_ref, DEEP)

    @pl.when(odd == 0)
    def _():
        fill(one, ADVECT, inter_ref, c_ref, intra_ref, 0)
        fill(force, ADVECT * FORCE, inter_ref, s_ref, intra_ref, DEEP)

    def tiles(first, last):
        upper = [low + 8 * i for i in range(first, last)]
        lower = [high + 8 * i for i in range(2 * third - last, 2 * third - first)]
        return upper + lower

    masks = {low + 8 * i: up_mask for i in range(third)}
    masks.update({high + HALO + 8 * i: down_mask for i in range(third)})

    def beside(target, piece):
        for n, at in enumerate((low + HALO + REACH, high + REACH)):
            for g in range(TILES):
                target[g, pl.ds(at, 8), :] = piece(n, g)

    def step(source, target, number):
        beside(source, lambda n, g: trace_ref[number - 1, n, g])
        sweep(source, target, force, tiles(1, 4), lane_ids, None, masks)

    sweep(one, two, force, tiles(0, 4), lane_ids, coarse, masks)
    step(two, one, 2)

    def pair(i, carry):
        step(one, two, 3 + 2 * i)
        step(two, one, 4 + 2 * i)
        return carry

    lax.fori_loop(0, STEPS // 2 - 1, pair, 0)
    beside(two, lambda n, g: inner_gift_ref[g, pl.ds(PAD + (REACH, ROWS - 2 * REACH)[n], 8), :])
    first = jnp.where(slab == 0, 0.0, 1.0)
    for at in tiles(1, 4):
        rows = pl.ds(at, 8)
        for g in range(TILES):
            fine = one[g, rows, :]
            rough = coarse[g, rows, :]
            if at in masks:
                rough = rough * masks[at]
            given = fine - first * rough
            two[g, rows, :] = given
            if at in (low + HALO, high + HALO - 8):
                cut = (pl.ds(0 if at == low + HALO else 8, 8), pl.ds(g * LANE, LANE))
                defect_ref[cut] = fine - rough
                rim_gift_ref[cut] = given
    for g in range(TILES):
        for i in range(2):
            rim_force_ref[g, pl.ds(8 * i, 8), :] = force[g, pl.ds(low + 8 + 8 * i, 8), :]
            rim_force_ref[g, pl.ds(16 + 8 * i, 8), :] = force[g, pl.ds(high + HALO + 8 * i, 8), :]
    ends = (low + HALO - FAR, high + HALO + FAR - PIECE)
    for order, out in ((0, mine_ref), (2, one_ref), (3, two_ref)):
        worker = slab ^ partner(order)

        def cut_rim(order=order, out=out):
            for n, start in enumerate(ends):
                for i in range(0, PIECE, 8):
                    size = min(8, PIECE - i)
                    for g in range(TILES):
                        rows = pl.ds(start + i, size)
                        out[pl.ds(BOX * g + PIECE * n + i, size), :] = two[g, rows, :]
                        if order == 0:
                            block_ref[g, pl.ds(PIECE * n + i, size), :] = force[g, rows, :]

        def cut_inner(order=order, out=out, worker=worker):
            start = PAD + inner_start(worker)
            for i in range(0, BLOCK, 8):
                for g in range(TILES):
                    rows = pl.ds(start + i, 8)
                    out[pl.ds(BOX * g + i, 8), :] = inner_gift_ref[g, rows, :]
                    if order == 0:
                        block_ref[g, pl.ds(i, 8), :] = inner_force_ref[g, rows, :]

        pl.when(worker == RIM_SLAB)(cut_rim)
        pl.when(worker != RIM_SLAB)(cut_inner)


def each_place(slab, odd, body):
    for t in range(SLABS):
        for core in range(2):
            pl.when((slab == t) & (odd == core))(functools.partial(body, t, ORDERS[core]))


def chain_kernel(mine_ref, one_ref, two_ref, three_ref, force_ref, out0_ref, out1_ref, out2_ref, out3_ref, start1, start2, start3):
    slab, odd, up_mask, down_mask = place()
    lane_ids = lanes()
    boxes = (mine_ref, one_ref, two_ref, three_ref)
    outs = (out0_ref, out1_ref, out2_ref, out3_ref)
    row_ids = lax.broadcasted_iota(jnp.int32, (8, LANE), 0)
    def mask_at(at):
        row = row_ids + at
        row = jnp.where(row < PIECE, row - FAR, row + (ROWS + FAR - BOX))
        return jnp.where(row < 0, up_mask, jnp.where(row >= ROWS, down_mask, 1.0))

    masks = {at: mask_at(at) for at in (0, 8, 32, BOX - 8)}

    def read(box, at, g):
        if box.shape[1] == COLS:
            return box[pl.ds(at, 8), pl.ds(g * LANE, LANE)]
        return box[pl.ds(BOX * g + at, 8), :]

    def leap(source, target, defect, tiles, rim):
        for at in tiles:
            for g, now, above, below, left, right in row_tile(source, PAD + at, lane_ids):
                inc = increment(now, above, below, left, right, force_ref[g, pl.ds(at, 8), :])
                new = now + 8.0 * inc + read(defect, at, g)
                target[g, pl.ds(PAD + at, 8), :] = new * masks[at] if rim and at in masks else new

    def body(t, order):
        rim = t == RIM_SLAB
        tiles = BOX_TILES if rim else BOX_TILES[: BLOCK // 8]
        for at in tiles:
            for g in range(TILES):
                start1[g, pl.ds(PAD + at, 8), :] = read(boxes[order.index(t)], at, g)
        leap(start1, start2, boxes[order.index(t ^ 1)], tiles, rim)
        leap(start2, start3, boxes[order.index(t ^ 2)], tiles, rim)
        starts = (None, start1, start2, start3)
        pieces = ((0, 2, EDGE), (EDGE, PIECE + 2, EDGE)) if rim else ((0, 2, PART),)
        for k in range(SLABS):
            begin = starts[max(t ^ order[k], 1)]
            for to, at, rows in pieces:
                for i in range(0, rows, 8):
                    size = min(8, rows - i)
                    for g in range(TILES):
                        outs[k][pl.ds(PART * g + to + i, size), :] = begin[g, pl.ds(PAD + at + i, size), :]

    each_place(slab, odd, body)


def first_kernel(inner_gift_ref, rim_gift_ref, inner_force_ref, rim_force_ref, new_out, end_out, wide_force, stage, sems):
    for g in range(TILES):
        for i in range(2):
            wide_force[g, pl.ds(8 * i, 8), :] = rim_force_ref[g, pl.ds(8 * i, 8), :]
            wide_force[g, pl.ds(16 + ROWS + 8 * i, 8), :] = rim_force_ref[g, pl.ds(16 + 8 * i, 8), :]
        for i in range(ROWS // 8):
            wide_force[g, pl.ds(16 + 8 * i, 8), :] = inner_force_ref[g, pl.ds(PAD + 8 * i, 8), :]

    @pl.when(lax.axis_index("tm") == 0)
    def _():
        last = ROWS // 8 - 1
        for g in range(TILES):
            cut = pl.ds(g * LANE, LANE)
            for i in range(last + 1):
                if i in (0, last):
                    value = rim_gift_ref[pl.ds(8 * (i > 0), 8), cut]
                else:
                    value = inner_gift_ref[g, pl.ds(PAD + 8 * i, 8), :]
                stage[pl.ds(8 * i, 8), cut] = value * (1.0 / ADVECT)
        copies = [pltpu.make_async_copy(stage, out, sems.at[n]) for n, out in enumerate((new_out, end_out))]
        for copy in copies:
            copy.start()
        for copy in copies:
            copy.wait()


def fine_kernel(*refs):
    pl.when(lax.axis_index("tm") > 0)(functools.partial(later_slabs, *refs))


def later_slabs(defect_ref, rim_defect_ref, force, mine_ref, one_ref, two_ref, three_ref, new_in, end_in, new_out, end_out, one, two, new_ref, end_ref, sems):
    boxes = (mine_ref, one_ref, two_ref, three_ref)
    slab, odd, up_mask, down_mask = place()
    lane_ids = lanes()
    base = PAD + REACH
    last = base + ROWS

    def body(t, order):
        for w in range(SLABS):
            source = boxes[order.index(t ^ w)]
            if w == RIM_SLAB:
                pieces = ((0, -REACH, EDGE), (EDGE, ROWS + REACH - EDGE, EDGE))
            else:
                pieces = ((0, EDGE - REACH + PART * (w - (w > RIM_SLAB)), PART),)
            for begin, row, rows in pieces:
                for i in range(0, rows, 8):
                    size = min(8, rows - i)
                    for g in range(TILES):
                        one[g, pl.ds(base + row + i, size), :] = source[pl.ds(PART * g + begin + i, size), :]

    each_place(slab, odd, body)

    tiles = [PAD + 8 * i for i in range((ROWS + 2 * REACH) // 8)]
    masks = {PAD: up_mask, last: down_mask}
    for at in tiles:
        for g, now, above, below, left, right in row_tile(one, at, lane_ids):
            inc = increment(now, above, below, left, right, force[g, pl.ds(at, 8), :])
            new = now + inc
            cut = pl.ds(g * LANE, LANE)
            if at in masks:
                new = new * masks[at]
            else:
                if at == base:
                    defect = rim_defect_ref[pl.ds(0, 8), cut]
                elif at == last - 8:
                    defect = rim_defect_ref[pl.ds(8, 8), cut]
                else:
                    defect = defect_ref[pl.ds(at - base, 8), cut]
                new_ref[pl.ds(at - base, 8), cut] = (now + 8.0 * inc + defect) * (1.0 / ADVECT)
            two[g, pl.ds(at, 8), :] = new

    copies = [pltpu.make_async_copy(new_ref, new_out, sems.at[0])]
    copies[0].start()

    def pair(_, carry):
        sweep(two, one, force, tiles, lane_ids, None, masks)
        sweep(one, two, force, tiles, lane_ids, None, masks)
        return carry

    lax.fori_loop(0, STEPS // 2 - 1, pair, 0)
    for at in tiles[1:-1]:
        for g, now, above, below, left, right in row_tile(two, at, lane_ids):
            inc = increment(now, above, below, left, right, force[g, pl.ds(at, 8), :])
            end_ref[pl.ds(at - base, 8), pl.ds(g * LANE, LANE)] = (now + inc) * (1.0 / ADVECT)
        done = at + 8 - base
        if done % CHUNK == 0:
            rows = pl.ds(done - CHUNK, CHUNK)
            copies.append(pltpu.make_async_copy(end_ref.at[rows], end_out.at[rows], sems.at[len(copies)]))
            copies[-1].start()
    for copy in copies:
        copy.wait()


def swap(array, axis, by):
    size = lax.axis_size(axis)
    return lax.ppermute(array, axis, [(i, i ^ by) for i in range(size)])


def swap_one(box, order):
    count, width = lax.axis_size("tm"), lax.axis_size("space")
    pairs = []
    for t in range(count):
        for strip in range(width):
            by = ORDERS[strip % 2][order]
            pairs.append((t * width + strip, (t ^ by) * width + strip))
    return lax.ppermute(box, ("tm", "space"), pairs)


def call(kernel, outs, scratch, place=pltpu.VMEM, copies=0, **more):
    places = place if isinstance(place, list) else [place] * len(outs)
    return pl.pallas_call(
        kernel,
        out_shape=[jax.ShapeDtypeStruct(shape, jnp.float32) for shape in outs],
        out_specs=[pl.BlockSpec(memory_space=space) for space in places],
        scratch_shapes=[pltpu.VMEM(shape, jnp.float32) for shape in scratch]
        + [pltpu.SemaphoreType.DMA((copies,))] * (copies > 0),
        compiler_params=pltpu.CompilerParams(vmem_limit_bytes=24 * 1024 * 1024),
        **more,
    )


def local(c_points, source):
    count = lax.axis_size("space")
    edges = (TILES * 2 * DEEP, LANE)
    field = c_points[0]
    to_inter, to_far, to_intra = call(pack_kernel, [edges, (FAR_BOX, COLS), edges], [])(field, source)
    pairs = []
    for t in range(lax.axis_size("tm")):
        for strip in range(count):
            if strip in (0, count - 1):
                mate = (t ^ 1) * count + strip
            else:
                mate = t * count + strip + (1 if strip % 2 else -1)
            pairs.append((t * count + strip, mate))
    inter = lax.ppermute(to_inter, ("tm", "space"), pairs)
    intra = swap(to_intra, "space", 1)

    wide = (TILES, ROWS + 2 * PAD, LANE)
    raw = swap_one(to_far, 1)
    defect, gift, force, trace = call(
        inner_kernel, [(ROWS, COLS), wide, wide, (STEPS + 1, 2, TILES, 8, LANE)], [wide] * 3
    )(field, source)
    narrow = (TILES, ROWS + 4 * REACH, LANE)
    box = (TILES * BOX, LANE)
    rim_defect, mine, one, two, block_force, rim_gift, rim_force = call(
        rim_kernel,
        [(16, COLS), box, box, box, (TILES, 48, LANE), (16, COLS), (TILES, 32, LANE)],
        [(TILES, 2 * SIDE, LANE)] * 4,
    )(field, source, intra, inter, gift, force, trace)
    one, two = swap_one(one, 2), swap_one(two, 3)
    far = call(far_kernel, [(BLOCK, COLS)], [(TILES, FAR_BOX + 2 * PAD, LANE)] * 4)(raw, force)[0]
    starts = call(
        chain_kernel, [(TILES * PART, LANE)] * 4, [(TILES, 48 + 2 * PAD, LANE)] * 3
    )(mine, far, one, two, block_force)
    starts = [starts[0]] + [swap_one(starts[order], order) for order in range(1, SLABS)]
    new, end, wide_force = call(
        first_kernel,
        [(ROWS, COLS), (ROWS, COLS), narrow],
        [(ROWS, COLS)],
        [pl.ANY, pl.ANY, pltpu.VMEM],
        2,
    )(gift, rim_gift, force, rim_force)
    middle = (TILES, ROWS + 2 * REACH + 2 * PAD, LANE)
    inside, outside = pl.BlockSpec(memory_space=pltpu.VMEM), pl.BlockSpec(memory_space=pl.ANY)
    corrected, fine = call(
        fine_kernel,
        [(ROWS, COLS)] * 2,
        [middle] * 2 + [(ROWS, COLS)] * 2,
        pl.ANY,
        1 + ROWS // CHUNK,
        in_specs=[inside] * 7 + [outside] * 2,
        input_output_aliases={7: 0, 8: 1},
    )(defect, rim_defect, wide_force, *starts, new, end)
    return corrected[None], fine[None]


def solution(mesh):
    return jax.shard_map(
        local,
        mesh=mesh,
        in_specs=(P("tm", "space", None), P("space", None)),
        out_specs=(P("tm", "space", None), P("tm", "space", None)),
        check_vma=False,
    )
```

```python
import functools

import jax
import jax.numpy as jnp
from jax import lax
from jax.experimental import pallas as pl
from jax.experimental.pallas import tpu as pltpu
from jax.sharding import PartitionSpec as P

ADVECT = 0.02
DIFFUSE = 0.01
FORCE = 0.05
STEPS = 8
SLABS = 4
ROWS = 128
COLS = 1024
LANE = 128
TILES = COLS // LANE
HALO = 24
DEEP = 18
PAD = 8
REACH = STEPS
PART = (ROWS + 2 * REACH) // SLABS
BLOCK = PART + 4
BOX = 44
FAR_BOX = BLOCK + 2 * REACH
CHUNK = 32
PIECE = BOX // 2
BOX_TILES = (0, 8, 16, 24, 32, BOX - 8)
EDGE = PART // 2
FAR = REACH + 2
RIM_SLAB = 1
RIM = 2 * HALO
SIDE = RIM + 2 * PAD


ORDERS = ((0, 2, 1, 3), (0, 2, 3, 1))


def increment(now, above, below, left, right, force):
    twice = now + now
    rear = above + left - twice
    ahead = below + right - twice
    gain = jnp.maximum(now, 0.0) + DIFFUSE
    return force + gain * rear + (gain - now) * ahead


def row_tile(state, start, lane_ids):
    now = [state[g, pl.ds(start, 8), :] for g in range(TILES)]
    above = [state[g, pl.ds(start - 1, 8), :] for g in range(TILES)]
    below = [state[g, pl.ds(start + 1, 8), :] for g in range(TILES)]
    for g in range(TILES):
        left = pltpu.roll(jnp.where(lane_ids == LANE - 1, now[g - 1], now[g]), 1, 1)
        right = pltpu.roll(jnp.where(lane_ids == 0, now[(g + 1) % TILES], now[g]), LANE - 1, 1)
        yield g, now[g], above[g], below[g], left, right


def lanes():
    return lax.broadcasted_iota(jnp.int32, (8, LANE), 1)


def parity():
    return lax.axis_index("space") % 2


def place():
    slab = lax.axis_index("tm")
    strip = lax.axis_index("space")
    up_mask = jnp.where(strip == 0, 0.0, 1.0)
    down_mask = jnp.where(strip == lax.axis_size("space") - 1, 0.0, 1.0)
    return slab, strip % 2, up_mask, down_mask


def pack_kernel(c_ref, s_ref, inter_ref, far_ref, intra_ref):
    odd = parity()

    def edges(core):
        top, bottom = 0, ROWS - DEEP
        for out, start in ((inter_ref, bottom if core else top), (intra_ref, top if core else bottom)):
            for n, source in enumerate((c_ref, s_ref)):
                for i in range(0, DEEP, 8):
                    size = min(8, DEEP - i)
                    for g in range(TILES):
                        piece = source[pl.ds(start + i, size), pl.ds(g * LANE, LANE)]
                        out[pl.ds(2 * DEEP * g + DEEP * n + i, size), :] = piece

    def inner(place):
        for i in range(0, FAR_BOX, 8):
            far_ref[pl.ds(i, 8), :] = c_ref[pl.ds(PART * place + i, 8), :]

    for core in range(2):
        pl.when(odd == core)(functools.partial(edges, core))
    wanted = inner_place(lax.axis_index("tm") ^ 2)
    for place in range(SLABS - 1):
        pl.when(wanted == place)(functools.partial(inner, place))


def load_deep(target, at, source, begin, scale):
    for i in range(0, DEEP, 8):
        size = min(8, DEEP - i)
        for g in range(TILES):
            target[g, pl.ds(at + i, size), :] = source[pl.ds(2 * DEEP * g + begin + i, size), :] * scale


def load(target, at, source, start, count, scale):
    for i in range(count):
        for g in range(TILES):
            target[g, pl.ds(at + 8 * i, 8), :] = source[pl.ds(start + 8 * i, 8), pl.ds(g * LANE, LANE)] * scale


def sweep(source, target, force, tiles, lane_ids, coarse=None, masks=None):
    for at in tiles:
        for g, now, above, below, left, right in row_tile(source, at, lane_ids):
            inc = increment(now, above, below, left, right, force[g, pl.ds(at, 8), :])
            new = now + inc
            if coarse is not None:
                coarse[g, pl.ds(at, 8), :] = now + 8.0 * inc
            if masks and at in masks:
                new = new * masks[at]
            target[g, pl.ds(at, 8), :] = new


def partner(place):
    first, second = ORDERS[0][place], ORDERS[1][place]
    return first if first == second else jnp.where(parity() == 0, first, second)


def inner_place(worker):
    return jnp.where(worker > RIM_SLAB, worker - 1, 0)


def inner_start(worker):
    return REACH + PART * inner_place(worker)


def inner_kernel(c_ref, s_ref, defect_ref, gift_ref, force_ref, trace_ref, one, two, coarse):
    slab = lax.axis_index("tm")
    lane_ids = lanes()
    count = ROWS // 8
    load(one, PAD, c_ref, 0, count, ADVECT)
    load(force_ref, PAD, s_ref, 0, count, ADVECT * FORCE)
    tiles = [PAD + 8 * i for i in range(count)]

    def note(step, state):
        for n, row in enumerate((REACH, ROWS - 2 * REACH)):
            for g in range(TILES):
                trace_ref[step, n, g] = state[g, pl.ds(PAD + row, 8), :]

    sweep(one, two, force_ref, tiles, lane_ids, coarse)
    note(1, two)
    sweep(two, one, force_ref, tiles, lane_ids)
    note(2, one)

    def pair(i, carry):
        sweep(one, two, force_ref, tiles, lane_ids)
        note(3 + 2 * i, two)
        sweep(two, one, force_ref, tiles, lane_ids)
        note(4 + 2 * i, one)
        return carry

    lax.fori_loop(0, STEPS // 2 - 1, pair, 0)
    first = jnp.where(slab == 0, 0.0, 1.0)
    for i in range(1, count - 1):
        rows = pl.ds(PAD + 8 * i, 8)
        for g in range(TILES):
            fine = one[g, rows, :]
            rough = coarse[g, rows, :]
            gift_ref[g, rows, :] = fine - first * rough
            defect_ref[pl.ds(8 * i, 8), pl.ds(g * LANE, LANE)] = fine - rough


def far_kernel(raw_ref, force_ref, far_ref, one, two, force, coarse):
    slab = lax.axis_index("tm")
    lane_ids = lanes()
    count = FAR_BOX // 8
    tiles = [PAD + 8 * i for i in range(count)]
    load(one, PAD, raw_ref, 0, count, ADVECT)
    low = PAD + PART * inner_place(slab)
    for g in range(TILES):
        for i in range(count):
            force[g, pl.ds(PAD + 8 * i, 8), :] = force_ref[g, pl.ds(low + 8 * i, 8), :]
    sweep(one, two, force, tiles, lane_ids, coarse)
    sweep(two, one, force, tiles, lane_ids)

    def pair(_, carry):
        sweep(one, two, force, tiles, lane_ids)
        sweep(two, one, force, tiles, lane_ids)
        return carry

    lax.fori_loop(0, STEPS // 2 - 1, pair, 0)
    first = jnp.where(slab ^ 2 == 0, 0.0, 1.0)
    start = PAD + REACH
    for i in range(BLOCK // 8):
        rows = pl.ds(start + 8 * i, 8)
        for g in range(TILES):
            far_ref[pl.ds(8 * i, 8), pl.ds(g * LANE, LANE)] = one[g, rows, :] - first * coarse[g, rows, :]


def rim_kernel(c_ref, s_ref, intra_ref, inter_ref, inner_gift_ref, inner_force_ref, trace_ref, defect_ref, mine_ref, one_ref, two_ref, block_ref, rim_gift_ref, rim_force_ref, one, two, force, coarse):
    slab, odd, up_mask, down_mask = place()
    lane_ids = lanes()
    low, high = PAD, SIDE + PAD
    third = HALO // 8

    def fill(target, scale, top, main, bottom, offset):
        load_deep(target, low + HALO - DEEP, top, offset, scale * up_mask)
        load(target, low + HALO, main, 0, third, scale)
        load(target, high, main, ROWS - HALO, third, scale)
        load_deep(target, high + HALO, bottom, offset, scale * down_mask)

    @pl.when(odd == 1)
    def _():
        fill(one, ADVECT, intra_ref, c_ref, inter_ref, 0)
        fill(force, ADVECT * FORCE, intra_ref, s_ref, inter_ref, DEEP)

    @pl.when(odd == 0)
    def _():
        fill(one, ADVECT, inter_ref, c_ref, intra_ref, 0)
        fill(force, ADVECT * FORCE, inter_ref, s_ref, intra_ref, DEEP)

    def tiles(first, last):
        upper = [low + 8 * i for i in range(first, last)]
        lower = [high + 8 * i for i in range(2 * third - last, 2 * third - first)]
        return upper + lower

    masks = {low + 8 * i: up_mask for i in range(third)}
    masks.update({high + HALO + 8 * i: down_mask for i in range(third)})

    def beside(target, piece):
        for n, at in enumerate((low + HALO + REACH, high + REACH)):
            for g in range(TILES):
                target[g, pl.ds(at, 8), :] = piece(n, g)

    def step(source, target, number):
        beside(source, lambda n, g: trace_ref[number - 1, n, g])
        sweep(source, target, force, tiles(1, 4), lane_ids, None, masks)

    sweep(one, two, force, tiles(0, 4), lane_ids, coarse, masks)
    step(two, one, 2)

    def pair(i, carry):
        step(one, two, 3 + 2 * i)
        step(two, one, 4 + 2 * i)
        return carry

    lax.fori_loop(0, STEPS // 2 - 1, pair, 0)
    beside(two, lambda n, g: inner_gift_ref[g, pl.ds(PAD + (REACH, ROWS - 2 * REACH)[n], 8), :])
    first = jnp.where(slab == 0, 0.0, 1.0)
    for at in tiles(1, 4):
        rows = pl.ds(at, 8)
        for g in range(TILES):
            fine = one[g, rows, :]
            rough = coarse[g, rows, :]
            if at in masks:
                rough = rough * masks[at]
            given = fine - first * rough
            two[g, rows, :] = given
            if at in (low + HALO, high + HALO - 8):
                cut = (pl.ds(0 if at == low + HALO else 8, 8), pl.ds(g * LANE, LANE))
                defect_ref[cut] = fine - rough
                rim_gift_ref[cut] = given
    for g in range(TILES):
        for i in range(2):
            rim_force_ref[g, pl.ds(8 * i, 8), :] = force[g, pl.ds(low + 8 + 8 * i, 8), :]
            rim_force_ref[g, pl.ds(16 + 8 * i, 8), :] = force[g, pl.ds(high + HALO + 8 * i, 8), :]
    ends = (low + HALO - FAR, high + HALO + FAR - PIECE)
    for order, out in ((0, mine_ref), (2, one_ref), (3, two_ref)):
        worker = slab ^ partner(order)

        def cut_rim(order=order, out=out):
            for n, start in enumerate(ends):
                for i in range(0, PIECE, 8):
                    size = min(8, PIECE - i)
                    for g in range(TILES):
                        rows = pl.ds(start + i, size)
                        out[pl.ds(BOX * g + PIECE * n + i, size), :] = two[g, rows, :]
                        if order == 0:
                            block_ref[g, pl.ds(PIECE * n + i, size), :] = force[g, rows, :]

        def cut_inner(order=order, out=out, worker=worker):
            start = PAD + inner_start(worker)
            for i in range(0, BLOCK, 8):
                for g in range(TILES):
                    rows = pl.ds(start + i, 8)
                    out[pl.ds(BOX * g + i, 8), :] = inner_gift_ref[g, rows, :]
                    if order == 0:
                        block_ref[g, pl.ds(i, 8), :] = inner_force_ref[g, rows, :]

        pl.when(worker == RIM_SLAB)(cut_rim)
        pl.when(worker != RIM_SLAB)(cut_inner)


def each_place(slab, odd, body):
    for t in range(SLABS):
        for core in range(2):
            pl.when((slab == t) & (odd == core))(functools.partial(body, t, ORDERS[core]))


def chain_kernel(mine_ref, one_ref, two_ref, three_ref, force_ref, out0_ref, out1_ref, out2_ref, out3_ref, start1, start2, start3):
    slab, odd, up_mask, down_mask = place()
    lane_ids = lanes()
    boxes = (mine_ref, one_ref, two_ref, three_ref)
    outs = (out0_ref, out1_ref, out2_ref, out3_ref)
    row_ids = lax.broadcasted_iota(jnp.int32, (8, LANE), 0)
    def mask_at(at):
        row = row_ids + at
        row = jnp.where(row < PIECE, row - FAR, row + (ROWS + FAR - BOX))
        return jnp.where(row < 0, up_mask, jnp.where(row >= ROWS, down_mask, 1.0))

    masks = {at: mask_at(at) for at in (0, 8, 32, BOX - 8)}

    def read(box, at, g):
        if box.shape[1] == COLS:
            return box[pl.ds(at, 8), pl.ds(g * LANE, LANE)]
        return box[pl.ds(BOX * g + at, 8), :]

    def leap(source, target, defect, tiles, rim):
        for at in tiles:
            for g, now, above, below, left, right in row_tile(source, PAD + at, lane_ids):
                inc = increment(now, above, below, left, right, force_ref[g, pl.ds(at, 8), :])
                new = now + 8.0 * inc + read(defect, at, g)
                target[g, pl.ds(PAD + at, 8), :] = new * masks[at] if rim and at in masks else new

    def body(t, order):
        rim = t == RIM_SLAB
        tiles = BOX_TILES if rim else BOX_TILES[: BLOCK // 8]
        for at in tiles:
            for g in range(TILES):
                start1[g, pl.ds(PAD + at, 8), :] = read(boxes[order.index(t)], at, g)
        leap(start1, start2, boxes[order.index(t ^ 1)], tiles, rim)
        leap(start2, start3, boxes[order.index(t ^ 2)], tiles, rim)
        starts = (None, start1, start2, start3)
        pieces = ((0, 2, EDGE), (EDGE, PIECE + 2, EDGE)) if rim else ((0, 2, PART),)
        for k in range(SLABS):
            begin = starts[max(t ^ order[k], 1)]
            for to, at, rows in pieces:
                for i in range(0, rows, 8):
                    size = min(8, rows - i)
                    for g in range(TILES):
                        outs[k][pl.ds(PART * g + to + i, size), :] = begin[g, pl.ds(PAD + at + i, size), :]

    each_place(slab, odd, body)


def first_kernel(inner_gift_ref, rim_gift_ref, inner_force_ref, rim_force_ref, new_out, end_out, wide_force, stage, sems):
    for g in range(TILES):
        for i in range(2):
            wide_force[g, pl.ds(8 * i, 8), :] = rim_force_ref[g, pl.ds(8 * i, 8), :]
            wide_force[g, pl.ds(16 + ROWS + 8 * i, 8), :] = rim_force_ref[g, pl.ds(16 + 8 * i, 8), :]
        for i in range(ROWS // 8):
            wide_force[g, pl.ds(16 + 8 * i, 8), :] = inner_force_ref[g, pl.ds(PAD + 8 * i, 8), :]

    @pl.when(lax.axis_index("tm") == 0)
    def _():
        last = ROWS // 8 - 1
        for g in range(TILES):
            cut = pl.ds(g * LANE, LANE)
            for i in range(last + 1):
                if i in (0, last):
                    value = rim_gift_ref[pl.ds(8 * (i > 0), 8), cut]
                else:
                    value = inner_gift_ref[g, pl.ds(PAD + 8 * i, 8), :]
                stage[pl.ds(8 * i, 8), cut] = value * (1.0 / ADVECT)
        copies = [pltpu.make_async_copy(stage, out, sems.at[n]) for n, out in enumerate((new_out, end_out))]
        for copy in copies:
            copy.start()
        for copy in copies:
            copy.wait()


def fine_kernel(*refs):
    pl.when(lax.axis_index("tm") > 0)(functools.partial(later_slabs, *refs))


def later_slabs(defect_ref, rim_defect_ref, force, mine_ref, one_ref, two_ref, three_ref, new_in, end_in, new_out, end_out, one, two, new_ref, end_ref, sems):
    boxes = (mine_ref, one_ref, two_ref, three_ref)
    slab, odd, up_mask, down_mask = place()
    lane_ids = lanes()
    base = PAD + REACH
    last = base + ROWS

    def body(t, order):
        for w in range(SLABS):
            source = boxes[order.index(t ^ w)]
            if w == RIM_SLAB:
                pieces = ((0, -REACH, EDGE), (EDGE, ROWS + REACH - EDGE, EDGE))
            else:
                pieces = ((0, EDGE - REACH + PART * (w - (w > RIM_SLAB)), PART),)
            for begin, row, rows in pieces:
                for i in range(0, rows, 8):
                    size = min(8, rows - i)
                    for g in range(TILES):
                        one[g, pl.ds(base + row + i, size), :] = source[pl.ds(PART * g + begin + i, size), :]

    each_place(slab, odd, body)

    tiles = [PAD + 8 * i for i in range((ROWS + 2 * REACH) // 8)]
    masks = {PAD: up_mask, last: down_mask}
    for at in tiles:
        for g, now, above, below, left, right in row_tile(one, at, lane_ids):
            inc = increment(now, above, below, left, right, force[g, pl.ds(at, 8), :])
            new = now + inc
            cut = pl.ds(g * LANE, LANE)
            if at in masks:
                new = new * masks[at]
            else:
                if at == base:
                    defect = rim_defect_ref[pl.ds(0, 8), cut]
                elif at == last - 8:
                    defect = rim_defect_ref[pl.ds(8, 8), cut]
                else:
                    defect = defect_ref[pl.ds(at - base, 8), cut]
                new_ref[pl.ds(at - base, 8), cut] = (now + 8.0 * inc + defect) * (1.0 / ADVECT)
            two[g, pl.ds(at, 8), :] = new

    copies = [pltpu.make_async_copy(new_ref, new_out, sems.at[0])]
    copies[0].start()

    def pair(_, carry):
        sweep(two, one, force, tiles, lane_ids, None, masks)
        sweep(one, two, force, tiles, lane_ids, None, masks)
        return carry

    lax.fori_loop(0, STEPS // 2 - 2, pair, 0)
    sweep(two, one, force, tiles, lane_ids, None, masks)
    sweep(one, two, force, tiles[:1], lane_ids, None, masks)
    for n, at in enumerate(tiles[1:]):
        sweep(one, two, force, [at], lane_ids, None, masks)
        at = tiles[n]
        if n == 0:
            continue
        for g, now, above, below, left, right in row_tile(two, at, lane_ids):
            inc = increment(now, above, below, left, right, force[g, pl.ds(at, 8), :])
            end_ref[pl.ds(at - base, 8), pl.ds(g * LANE, LANE)] = (now + inc) * (1.0 / ADVECT)
        done = at + 8 - base
        if done % CHUNK == 0:
            rows = pl.ds(done - CHUNK, CHUNK)
            copies.append(pltpu.make_async_copy(end_ref.at[rows], end_out.at[rows], sems.at[len(copies)]))
            copies[-1].start()
    for copy in copies:
        copy.wait()


def swap(array, axis, by):
    size = lax.axis_size(axis)
    return lax.ppermute(array, axis, [(i, i ^ by) for i in range(size)])


def swap_one(box, order):
    count, width = lax.axis_size("tm"), lax.axis_size("space")
    pairs = []
    for t in range(count):
        for strip in range(width):
            by = ORDERS[strip % 2][order]
            pairs.append((t * width + strip, (t ^ by) * width + strip))
    return lax.ppermute(box, ("tm", "space"), pairs)


def call(kernel, outs, scratch, place=pltpu.VMEM, copies=0, **more):
    places = place if isinstance(place, list) else [place] * len(outs)
    return pl.pallas_call(
        kernel,
        out_shape=[jax.ShapeDtypeStruct(shape, jnp.float32) for shape in outs],
        out_specs=[pl.BlockSpec(memory_space=space) for space in places],
        scratch_shapes=[pltpu.VMEM(shape, jnp.float32) for shape in scratch]
        + [pltpu.SemaphoreType.DMA((copies,))] * (copies > 0),
        compiler_params=pltpu.CompilerParams(vmem_limit_bytes=24 * 1024 * 1024),
        **more,
    )


def local(c_points, source):
    count = lax.axis_size("space")
    edges = (TILES * 2 * DEEP, LANE)
    field = c_points[0]
    to_inter, to_far, to_intra = call(pack_kernel, [edges, (FAR_BOX, COLS), edges], [])(field, source)
    pairs = []
    for t in range(lax.axis_size("tm")):
        for strip in range(count):
            if strip in (0, count - 1):
                mate = (t ^ 1) * count + strip
            else:
                mate = t * count + strip + (1 if strip % 2 else -1)
            pairs.append((t * count + strip, mate))
    inter = lax.ppermute(to_inter, ("tm", "space"), pairs)
    intra = swap(to_intra, "space", 1)

    wide = (TILES, ROWS + 2 * PAD, LANE)
    raw = swap_one(to_far, 1)
    defect, gift, force, trace = call(
        inner_kernel, [(ROWS, COLS), wide, wide, (STEPS + 1, 2, TILES, 8, LANE)], [wide] * 3
    )(field, source)
    narrow = (TILES, ROWS + 4 * REACH, LANE)
    box = (TILES * BOX, LANE)
    rim_defect, mine, one, two, block_force, rim_gift, rim_force = call(
        rim_kernel,
        [(16, COLS), box, box, box, (TILES, 48, LANE), (16, COLS), (TILES, 32, LANE)],
        [(TILES, 2 * SIDE, LANE)] * 4,
    )(field, source, intra, inter, gift, force, trace)
    one, two = swap_one(one, 2), swap_one(two, 3)
    far = call(far_kernel, [(BLOCK, COLS)], [(TILES, FAR_BOX + 2 * PAD, LANE)] * 4)(raw, force)[0]
    starts = call(
        chain_kernel, [(TILES * PART, LANE)] * 4, [(TILES, 48 + 2 * PAD, LANE)] * 3
    )(mine, far, one, two, block_force)
    starts = [starts[0]] + [swap_one(starts[order], order) for order in range(1, SLABS)]
    new, end, wide_force = call(
        first_kernel,
        [(ROWS, COLS), (ROWS, COLS), narrow],
        [(ROWS, COLS)],
        [pl.ANY, pl.ANY, pltpu.VMEM],
        2,
    )(gift, rim_gift, force, rim_force)
    middle = (TILES, ROWS + 2 * REACH + 2 * PAD, LANE)
    inside, outside = pl.BlockSpec(memory_space=pltpu.VMEM), pl.BlockSpec(memory_space=pl.ANY)
    corrected, fine = call(
        fine_kernel,
        [(ROWS, COLS)] * 2,
        [middle] * 2 + [(ROWS, COLS)] * 2,
        pl.ANY,
        1 + ROWS // CHUNK,
        in_specs=[inside] * 7 + [outside] * 2,
        input_output_aliases={7: 0, 8: 1},
    )(defect, rim_defect, wide_force, *starts, new, end)
    return corrected[None], fine[None]


def solution(mesh):
    return jax.shard_map(
        local,
        mesh=mesh,
        in_specs=(P("tm", "space", None), P("space", None)),
        out_specs=(P("tm", "space", None), P("tm", "space", None)),
        check_vma=False,
    )
```
